512 devices in a mesh: seq: 32 (over x, z), chan: 16 (over y, core).
Axes of the slice: x: 4, y: 8, z: 8, core: 2. Of those that a mesh axis runs over, the one named last changes fastest.
Arguments:
- query_feat: bfloat16 [16384, 8192], P('seq', 'chan'), may hold values from -6 to 6
- key_feat: bfloat16 [16384, 8192], P('seq', 'chan'), may hold values from -6 to 6
- value_feat: bfloat16 [16384, 8192], P('seq', 'chan'), may hold values from -6 to 6
- decay_rate: float32 [8, 8192], P(None, 'chan'), may hold values from 1e-05 to 0.05
- residues: float32 [8, 8192], P(None, 'chan'), may hold values from -4 to 4
- skip_gain: float32 [8192], P('chan'), may hold values from -1 to 1
- norm_gain: float32 [8192], P('chan'), may hold values from 0.25 to 1.75
- doc_starts: int32 [256], replicated, may hold values from 0 to 1, as said below
- cotangent: bfloat16 [16384, 8192], P('seq', 'chan'), may hold values from -6 to 6
Outputs:
- mixed: bfloat16 [16384, 8192], P('seq', 'chan')
- grad_query: bfloat16 [16384, 8192], P('seq', 'chan')
- grad_key: bfloat16 [16384, 8192], P('seq', 'chan')
- grad_value: bfloat16 [16384, 8192], P('seq', 'chan')
The draws below stay inside these ranges and needn't reach their ends.
Inputs may be any that keep to these rules, and one draw needn't show every extreme that they name: doc_starts[0] is 1; a 1 at tile i means a document starts at token 64 * i.
All inputs are finite; a program needn't handle non-finite values.
Results may differ from the reference program's by a relative error of at most 0.0057.
Values may be sent and summed in bfloat16 or wider, within the bound.
No kernel may reach another device: no remote copies, remote signals or barrier semaphores. Data moves between devices by JAX's collectives and lax.ppermute only.
A program may use at most 128 MiB of HBM per device.

```python
import math
import jax
import jax.numpy as jnp
from jax import lax

D = 8192
MODES = 8
TILE = 64
TOKENS = 16384
NTILES = 256


def draw_doc_starts(key, part):
    key = jax.random.fold_in(key, 7)
    rolls = jax.random.randint(key, (NTILES,), 0, max(2, NTILES // 8))
    flags = (rolls == 0).astype(jnp.int32)
    return flags.at[0].set(1)


def shard_levels(key, dims, cuts, smallest, high):
    def one(axis_at, blocks):
        draws = jax.random.uniform(jax.random.fold_in(jax.random.fold_in(key, 6), axis_at), (blocks,), jnp.float32, smallest / len(cuts), high / len(cuts))
        return jnp.repeat(jnp.exp(draws), dims[axis_at] // blocks).reshape((-1,) + (1,) * (len(dims) - axis_at - 1))

    gain = one(*cuts[0])
    for cut in cuts[1:]:
        gain = gain * one(*cut)
    return gain


def normal_values(own_key, dims, spread, limit, cuts=(), kind=jnp.bfloat16):
    drawn = spread * jax.random.normal(own_key, dims, jnp.float32)
    if cuts:
        drawn = drawn * shard_levels(own_key, dims, cuts, -0.22, 0.18)
    return jnp.clip(drawn, -limit, limit).astype(kind)


def setup_inputs(seed: int = 0) -> dict:
    splits = jax.random.split(jax.random.key(seed), 10)
    return {
        "query_feat": normal_values(splits[0], (TOKENS, D), 1.0, 6.0, ((0, 32), (1, 16))),
        "key_feat": normal_values(splits[1], (TOKENS, D), 1.0, 6.0, ((0, 32), (1, 16))),
        "value_feat": normal_values(splits[2], (TOKENS, D), 1.0, 6.0, ((0, 32), (1, 16))),
        "decay_rate": jnp.clip(jnp.exp(math.log(0.05) - 8.517193 * jax.random.uniform(splits[3], (MODES, D), jnp.float32) ** shard_levels(splits[3], (MODES, D), ((1, 16),), -0.2, 0.2)), 9.999999747378752e-06, 0.05),
        "residues": normal_values(splits[4], (MODES, D), 1.0, 4.0, ((1, 16),), jnp.float32),
        "skip_gain": jnp.clip(jax.random.uniform(splits[5], (D,), jnp.float32, -1.0, 1.0) * shard_levels(splits[5], (D,), ((0, 16),), -0.4, 0.0), -1.0, 1.0),
        "norm_gain": jnp.clip(1.0 + 0.15 * jax.random.normal(splits[6], (D,), jnp.float32), 0.25, 1.75),
        "doc_starts": draw_doc_starts(jax.random.fold_in(splits[9], 71), 0),
        "cotangent": normal_values(splits[8], (TOKENS, D), 1.0, 6.0, ((0, 32), (1, 16))),
    }


highest = lax.Precision.HIGHEST

def compose(earlier, later):
    return (earlier[0] * later[0], later[0] * earlier[1] + later[1])

def make_tables(rate, weight):
    offsets = jnp.arange(TILE, dtype=jnp.float32)
    mode_weight = weight * jnp.sqrt(-jnp.expm1(-2.0 * rate))
    powers = jnp.exp(-rate[:, :, None] * offsets)
    kernel = lax.optimization_barrier(jnp.sum(mode_weight[:, :, None] * powers, axis=0))
    lag_index = jnp.arange(TILE)[:, None] - jnp.arange(TILE)[None, :]
    toeplitz = jnp.where(lag_index >= 0, kernel[:, jnp.clip(lag_index, 0, TILE - 1)], 0.0)
    tail_decay = jnp.exp(-rate[:, :, None] * (TILE - 1.0 - offsets))
    head_decay = mode_weight[:, :, None] * jnp.exp(-rate[:, :, None] * (offsets + 1.0))
    back_decay = mode_weight[:, :, None] * jnp.exp(-rate[:, :, None] * (TILE - offsets))
    tile_decay = jnp.exp(-rate * TILE)
    return (toeplitz, powers, tail_decay, head_decay, back_decay, tile_decay)

def forward_local(tile_data, survive, tables):
    toeplitz, powers, tail_decay, head_decay, back_decay, tile_decay = tables
    inside = jnp.einsum('cts,nsc->ntc', toeplitz, tile_data, precision=highest)
    ends = jnp.einsum('mcs,nsc->nmc', tail_decay, tile_data, precision=highest)
    decay = tile_decay[None] * survive[:, None, None]
    decay_total, state_total = lax.associative_scan(compose, (decay, ends))
    return (inside, decay_total, state_total)

def forward_finish(inside, decay_total, state_total, survive, head_decay, incoming):
    full = state_total + decay_total * incoming
    entering = jnp.concatenate([incoming[None], full[:-1]], axis=0) * survive[:, None, None]
    return inside + jnp.einsum('mcs,nmc->nsc', head_decay, entering, precision=highest)

def backward_local(tile_data, survive, tables):
    toeplitz, powers, tail_decay, head_decay, back_decay, tile_decay = tables
    inside = jnp.einsum('cts,ntc->nsc', toeplitz, tile_data, precision=highest)
    fronts = jnp.einsum('mcs,nsc->nmc', powers, tile_data, precision=highest)
    decay = tile_decay[None] * survive[:, None, None]
    gated = fronts * survive[:, None, None]
    decay_total, state_total = lax.associative_scan(compose, (jnp.flip(decay, 0), jnp.flip(gated, 0)))
    return (inside, jnp.flip(decay_total, 0), jnp.flip(state_total, 0))

def backward_finish(inside, decay_total, state_total, back_decay, incoming):
    full = state_total + decay_total * incoming
    arriving = jnp.concatenate([full[1:], incoming[None]], axis=0)
    return inside + jnp.einsum('mcs,nmc->nsc', back_decay, arriving, precision=highest)

def reference(query_feat, key_feat, value_feat, decay_rate, residues, skip_gain, norm_gain, doc_starts, cotangent):
    survive = (1 - doc_starts).astype(jnp.float32)
    group = 512 if D % 512 == 0 else D
    count = D // group

    def split(array):
        return jnp.moveaxis(array.reshape(array.shape[0], count, group), 1, 0)

    def join(array):
        return jnp.moveaxis(array, 0, 1).reshape(array.shape[1], D)
    product = (key_feat.astype(jnp.float32) * value_feat.astype(jnp.float32)).astype(jnp.bfloat16)
    rate_groups = split(decay_rate)
    weight_groups = split(residues)
    skip_groups = split(skip_gain[None])[:, 0]

    def forward_group(pieces):
        source, rate, weight, skip = pieces
        tables = make_tables(rate, weight)
        tile_data = source.astype(jnp.float32).reshape(NTILES, TILE, group)
        inside, decay_total, state_total = forward_local(tile_data, survive, tables)
        nothing = jnp.zeros(rate.shape, jnp.float32)
        conv = forward_finish(inside, decay_total, state_total, survive, tables[3], nothing).reshape(TOKENS, group)
        return (conv + skip * source.astype(jnp.float32)).astype(jnp.bfloat16)
    mixer = join(lax.map(forward_group, (split(product), rate_groups, weight_groups, skip_groups)))
    gated = query_feat.astype(jnp.float32) * mixer.astype(jnp.float32)
    rinv = lax.rsqrt(lax.optimization_barrier(jnp.mean(gated * gated, axis=1)) + 1e-05)
    mixed = (gated * rinv[:, None] * norm_gain).astype(jnp.bfloat16)
    scaled = cotangent.astype(jnp.float32) * norm_gain
    inner_sum = lax.optimization_barrier(jnp.sum(scaled * gated, axis=1))
    dgated = rinv[:, None] * scaled - gated * (rinv ** 3 * inner_sum / D)[:, None]
    grad_query = (dgated * mixer.astype(jnp.float32)).astype(jnp.bfloat16)
    adjoint = (dgated * query_feat.astype(jnp.float32)).astype(jnp.bfloat16)

    def backward_group(pieces):
        source, rate, weight, skip = pieces
        tables = make_tables(rate, weight)
        tile_data = source.astype(jnp.float32).reshape(NTILES, TILE, group)
        inside, decay_total, state_total = backward_local(tile_data, survive, tables)
        nothing = jnp.zeros(rate.shape, jnp.float32)
        conv = backward_finish(inside, decay_total, state_total, tables[4], nothing).reshape(TOKENS, group)
        return (conv + skip * source.astype(jnp.float32)).astype(jnp.bfloat16)
    dproduct = join(lax.map(backward_group, (split(adjoint), rate_groups, weight_groups, skip_groups)))
    grad_key = (dproduct.astype(jnp.float32) * value_feat.astype(jnp.float32)).astype(jnp.bfloat16)
    grad_value = (dproduct.astype(jnp.float32) * key_feat.astype(jnp.float32)).astype(jnp.bfloat16)
    return (mixed, grad_query, grad_key, grad_value)
```

```python
import functools

import jax
import jax.numpy as jnp
from jax import lax
from jax.experimental import pallas as pl
from jax.experimental.pallas import tpu as pltpu
from jax.sharding import PartitionSpec as P

D = 8192
MODES = 8
TILE = 64
LANES = 128
F32 = jnp.float32
BF16 = jnp.bfloat16
HIGHEST = lax.Precision.HIGHEST
UNROLL = 8


def pack_state(state, dtype):
    half = state.shape[1] // 2
    return jnp.concatenate([state[:, :half], state[:, half:]], axis=0).astype(dtype)


def unpack_state(block):
    block = block.astype(F32)
    return jnp.concatenate([block[:MODES], block[MODES:]], axis=1)


def flag_sum(starts_ref, first, count):
    total = starts_ref[first]
    for step in range(1, count):
        total = total + starts_ref[first + step]
    return total


def survive(starts_ref, index):
    return (1 - starts_ref[index]).astype(F32)


def lane_group(group):
    return slice(group * LANES, (group + 1) * LANES)


def tile_states(data_ref, rate, ends_ref, tiles, groups, reverse):
    decay = jnp.exp(-rate)
    for group in range(groups):
        lanes = lane_group(group)
        factors = [
            jnp.broadcast_to(decay[m : m + 1, lanes], (tiles, LANES)) for m in range(MODES)
        ]

        def step(index, states):
            token = TILE - 1 - index if reverse else index
            x = data_ref[group, pl.ds(token, tiles, stride=TILE), :]
            return tuple(f * s + x for f, s in zip(factors, states))

        zero = jnp.zeros((tiles, LANES), F32)
        states = lax.fori_loop(0, TILE, step, (zero,) * MODES, unroll=UNROLL)
        for m in range(MODES):
            ends_ref[group, pl.ds(m, tiles, stride=MODES), :] = states[m]


def recur(data_ref, out_ref, rate, weight, skip, enter_ref, tiles, groups, reverse):
    decay = jnp.exp(-rate)
    for group in range(groups):
        lanes = lane_group(group)
        factors = [
            jnp.broadcast_to(decay[m : m + 1, lanes], (tiles, LANES)) for m in range(MODES)
        ]
        weights = [
            jnp.broadcast_to(weight[m : m + 1, lanes], (tiles, LANES)) for m in range(MODES)
        ]
        gain = jnp.broadcast_to(skip[:, lanes], (tiles, LANES))

        def step(index, states):
            token = TILE - 1 - index if reverse else index
            rows = pl.ds(token, tiles, stride=TILE)
            x = data_ref[group, rows, :]
            states = tuple(f * s + x for f, s in zip(factors, states))
            parts = [w * s for w, s in zip(weights, states)]
            while len(parts) > 1:
                parts = [a + b for a, b in zip(parts[::2], parts[1::2])]
            out_ref[group, rows, :] = parts[0] + gain * x
            return states

        first = tuple(enter_ref[group, pl.ds(m, tiles, stride=MODES), :] for m in range(MODES))
        lax.fori_loop(0, TILE, step, first, unroll=UNROLL)


def load(ref, rows=slice(None)):
    return jnp.concatenate([ref[group, rows, :] for group in range(ref.shape[0])], axis=1)


def store(ref, value, rows=slice(None)):
    for group in range(ref.shape[0]):
        ref[group, rows, :] = value[:, lane_group(group)]


def rows_of(tile):
    return slice(tile * MODES, (tile + 1) * MODES)


def first_kernel(parts, starts_ref, key_ref, value_ref, rate_ref, send_ref, ends_ref, data_ref):
    tokens, width = key_ref.shape
    tiles, groups = tokens // TILE, width // LANES
    me = lax.axis_index("seq")
    rate = rate_ref[...]
    product = key_ref[...].astype(F32) * value_ref[...].astype(F32)
    store(data_ref, product.astype(BF16).astype(F32))
    tile_states(data_ref, rate, ends_ref, tiles, groups, False)
    tile_decay = jnp.exp(-rate * TILE)
    full = load(ends_ref, rows_of(0))
    for tile in range(1, tiles):
        alive = survive(starts_ref, me * tiles + tile)
        full = load(ends_ref, rows_of(tile)) + tile_decay * alive * full
    block = pack_state(full, send_ref.dtype)
    for other in range(parts):
        send_ref[other] = block


def token_sums(array):
    total = array[:, :LANES]
    for group in range(1, array.shape[1] // LANES):
        total = total + array[:, lane_group(group)]
    ones = jnp.ones((8, LANES), F32)
    return [
        lax.dot_general(
            ones,
            total[block * LANES : (block + 1) * LANES],
            (((1,), (1,)), ((), ())),
            precision=HIGHEST,
            preferred_element_type=F32,
        )
        for block in range(array.shape[0] // LANES)
    ]


def second_kernel(
    parts,
    peers,
    starts_ref,
    key_ref,
    value_ref,
    query_ref,
    cot_ref,
    rate_ref,
    weight_ref,
    skip_ref,
    gain_ref,
    got_ref,
    ends_ref,
    mixer_ref,
    sums_ref,
    data_ref,
    conv_ref,
    enter_ref,
):
    tokens, width = key_ref.shape
    tiles, groups = tokens // TILE, width // LANES
    me = lax.axis_index("seq")
    rate = rate_ref[...]
    product = key_ref[...].astype(F32) * value_ref[...].astype(F32)
    store(data_ref, product.astype(BF16).astype(F32))
    tile_decay = jnp.exp(-rate * TILE)
    part_decay = jnp.exp(-rate * tokens)
    state = jnp.zeros_like(rate)
    for part in range(parts - 1):
        kept = jnp.where(flag_sum(starts_ref, part * tiles, tiles) == 0, 1.0, 0.0)
        later = unpack_state(got_ref[part]) + part_decay * kept * state
        state = jnp.where(part < me, later, state)
    for tile in range(tiles):
        enter = state * survive(starts_ref, me * tiles + tile)
        store(enter_ref, enter, rows_of(tile))
        state = load(ends_ref, rows_of(tile)) + tile_decay * enter
    recur(data_ref, conv_ref, rate, weight_ref[...], skip_ref[...], enter_ref, tiles, groups, False)
    mixer = load(conv_ref).astype(BF16)
    mixer_ref[...] = mixer
    gated = query_ref[...].astype(F32) * mixer.astype(F32)
    scaled = cot_ref[...].astype(F32) * gain_ref[...]
    rows = token_sums(gated * gated) + token_sums(scaled * gated)
    row = lax.broadcasted_iota(jnp.int32, (8, LANES), 0)
    block = rows[0]
    for index in range(1, len(rows)):
        block = jnp.where(row == index, rows[index], block)
    for other in range(peers):
        sums_ref[other] = block


def spread_row(array, row):
    return jnp.broadcast_to(jnp.transpose(array)[:, row : row + 1], (LANES, LANES))


def third_kernel(
    parts,
    peers,
    starts_ref,
    query_ref,
    cot_ref,
    mixer_ref,
    rate_ref,
    gain_ref,
    sums_ref,
    mixed_ref,
    grad_query_ref,
    adjoint_ref,
    send_ref,
    fronts_ref,
    data_ref,
):
    tokens, width = query_ref.shape
    tiles, groups = tokens // TILE, width // LANES
    blocks = tokens // LANES
    me = lax.axis_index("seq")
    rate = rate_ref[...]
    sums = sums_ref[0]
    for other in range(1, peers):
        sums = sums + sums_ref[other]
    rinv = lax.rsqrt(sums / D + 1e-05)
    lean = jnp.concatenate([sums[blocks:], sums[:blocks]], axis=0)
    lean = rinv * rinv * rinv * lean / D
    for block in range(blocks):
        rows = slice(block * LANES, (block + 1) * LANES)
        scale = jnp.tile(spread_row(rinv, block), (1, groups))
        shift = jnp.tile(spread_row(lean, block), (1, groups))
        query = query_ref[rows, :].astype(F32)
        mixer = mixer_ref[rows, :].astype(F32)
        gain = gain_ref[...]
        gated = query * mixer
        scaled = cot_ref[rows, :].astype(F32) * gain
        mixed_ref[rows, :] = (gated * scale * gain).astype(BF16)
        dgated = scale * scaled - gated * shift
        grad_query_ref[rows, :] = (dgated * mixer).astype(BF16)
        adjoint = (dgated * query).astype(BF16)
        adjoint_ref[rows, :] = adjoint
        store(data_ref, adjoint.astype(F32), rows)
    tile_states(data_ref, rate, fronts_ref, tiles, groups, True)
    tile_decay = jnp.exp(-rate * TILE)
    full = load(fronts_ref, rows_of(tiles - 1))
    for tile in range(tiles - 2, -1, -1):
        alive = survive(starts_ref, me * tiles + tile + 1)
        full = load(fronts_ref, rows_of(tile)) + tile_decay * alive * full
    block = pack_state(full, send_ref.dtype)
    for other in range(parts):
        send_ref[other] = block


def fourth_kernel(
    parts,
    starts_ref,
    key_ref,
    value_ref,
    adjoint_ref,
    rate_ref,
    weight_ref,
    skip_ref,
    got_ref,
    fronts_ref,
    grad_key_ref,
    grad_value_ref,
    data_ref,
    conv_ref,
    enter_ref,
):
    tokens, width = key_ref.shape
    tiles, groups = tokens // TILE, width // LANES
    me = lax.axis_index("seq")
    rate = rate_ref[...]
    store(data_ref, adjoint_ref[...].astype(F32))
    tile_decay = jnp.exp(-rate * TILE)
    part_decay = jnp.exp(-rate * tokens)
    state = jnp.zeros_like(rate)
    for part in range(parts - 1, 0, -1):
        first = part * tiles
        kept = jnp.where(flag_sum(starts_ref, first + 1, tiles - 1) == 0, 1.0, 0.0)
        later = (unpack_state(got_ref[part]) + part_decay * kept * state) * survive(starts_ref, first)
        state = jnp.where(part > me, later, state)
    for tile in range(tiles - 1, -1, -1):
        store(enter_ref, state, rows_of(tile))
        if tile:
            state = load(fronts_ref, rows_of(tile)) + tile_decay * state
            state = state * survive(starts_ref, me * tiles + tile)
    recur(data_ref, conv_ref, rate, weight_ref[...], skip_ref[...], enter_ref, tiles, groups, True)
    dproduct = load(conv_ref).astype(BF16).astype(F32)
    grad_key_ref[...] = (dproduct * value_ref[...].astype(F32)).astype(BF16)
    grad_value_ref[...] = (dproduct * key_ref[...].astype(F32)).astype(BF16)


def call(kernel, ins, outs, scratch, cost):
    return pl.pallas_call(
        kernel,
        out_shape=[jax.ShapeDtypeStruct(shape, dtype) for shape, dtype in outs],
        in_specs=[pl.BlockSpec(memory_space=space) for _, space in ins],
        out_specs=[pl.BlockSpec(memory_space=pltpu.VMEM) for _ in outs],
        scratch_shapes=[pltpu.VMEM(shape, F32) for shape in scratch],
        compiler_params=pltpu.CompilerParams(vmem_limit_bytes=40 * 1024 * 1024),
        cost_estimate=pl.CostEstimate(flops=cost, bytes_accessed=cost // 8, transcendentals=0),
    )(*[array for array, _ in ins])


STATE_TYPE = F32


def on_device(
    query_feat,
    key_feat,
    value_feat,
    decay_rate,
    residues,
    skip_gain,
    norm_gain,
    doc_starts,
    cotangent,
):
    tokens, width = query_feat.shape
    parts, peers = lax.axis_size("seq"), lax.axis_size("chan")
    tiles = tokens // TILE
    vmem = lambda array: (array, pltpu.VMEM)
    starts = (doc_starts, pltpu.SMEM)
    weight = residues * jnp.sqrt(-jnp.expm1(-2.0 * decay_rate))
    skip, gain = skip_gain[None], norm_gain[None]
    whole = (tokens, width)
    split, states = (
        (width // LANES, tokens, LANES),
        (width // LANES, tiles * MODES, LANES),
    )
    block = (parts, 2 * MODES, width // 2)
    work = tokens * width

    send, ends = call(
        functools.partial(first_kernel, parts),
        [starts, vmem(key_feat), vmem(value_feat), vmem(decay_rate)],
        [(block, STATE_TYPE), (states, F32)],
        [split],
        work * 20,
    )
    got = lax.all_to_all(send, "seq", 0, 0)
    mixer, sums = call(
        functools.partial(second_kernel, parts, peers),
        [starts]
        + [
            vmem(array)
            for array in (
                key_feat,
                value_feat,
                query_feat,
                cotangent,
                decay_rate,
                weight,
                skip,
                gain,
                got,
                ends,
            )
        ],
        [(whole, BF16), ((peers, 8, LANES), F32)],
        [split, split, states],
        work * 50,
    )
    sums = lax.all_to_all(sums, "chan", 0, 0)
    mixed, grad_query, adjoint, send, fronts = call(
        functools.partial(third_kernel, parts, peers),
        [starts]
        + [vmem(array) for array in (query_feat, cotangent, mixer, decay_rate, gain, sums)],
        [(whole, BF16), (whole, BF16), (whole, BF16), (block, STATE_TYPE), (states, F32)],
        [split],
        work * 40,
    )
    got = lax.all_to_all(send, "seq", 0, 0)
    grad_key, grad_value = call(
        functools.partial(fourth_kernel, parts),
        [starts]
        + [
            vmem(array)
            for array in (key_feat, value_feat, adjoint, decay_rate, weight, skip, got, fronts)
        ],
        [(whole, BF16), (whole, BF16)],
        [split, split, states],
        work * 50,
    )
    return mixed, grad_query, grad_key, grad_value


def solution(mesh):
    both = P("seq", "chan")
    in_specs = (
        both,
        both,
        both,
        P(None, "chan"),
        P(None, "chan"),
        P("chan"),
        P("chan"),
        P(),
        both,
    )
    return jax.shard_map(
        on_device, mesh=mesh, in_specs=in_specs, out_specs=(both,) * 4, check_vma=False
    )
```

```python
import functools

import jax
import jax.numpy as jnp
from jax import lax
from jax.experimental import pallas as pl
from jax.experimental.pallas import tpu as pltpu
from jax.sharding import PartitionSpec as P


D = 8192
MODES = 8
TILE = 64
LANES = 128
F32 = jnp.float32
BF16 = jnp.bfloat16
HIGHEST = lax.Precision.HIGHEST
UNROLL = 8
SEND = BF16


def rounded(array):
    return array.astype(BF16).astype(F32)


def lane_group(group):
    return slice(group * LANES, (group + 1) * LANES)


def survive(starts_ref, index):
    return (1 - starts_ref[index]).astype(F32)


def keeps(starts_ref, first, count):
    total = starts_ref[first]
    for step in range(1, count):
        total = total + starts_ref[first + step]
    return jnp.where(total == 0, 1.0, 0.0)


def rows_of(tile):
    return slice(tile * MODES, (tile + 1) * MODES)


def woven(offset, tiles):
    return pl.ds(pl.multiple_of(offset * tiles, tiles), tiles)


def over_tile(step, first, reverse):
    def body(index, carry):
        return step(TILE - 1 - index if reverse else index, carry)

    return lax.fori_loop(0, TILE, body, first, unroll=UNROLL)


def per_mode(table, tiles):
    return [jnp.broadcast_to(table[m : m + 1], (tiles, LANES)) for m in range(MODES)]


def total(parts):
    parts = list(parts)
    while len(parts) > 1:
        parts = [sum(parts[i : i + 2][1:], parts[i]) for i in range(0, len(parts), 2)]
    return parts[0]


def advance(factors, states, x):
    return tuple(f * s + x for f, s in zip(factors, states))


def put_states(ref, group, states, tiles):
    for m in range(MODES):
        ref[group, pl.ds(m, tiles, stride=MODES), :] = states[m]


def get_states(ref, group, tiles):
    return tuple(ref[group, pl.ds(m, tiles, stride=MODES), :] for m in range(MODES))


def send_state(states, send_ref):
    block = jnp.concatenate(states, axis=0).astype(send_ref.dtype)
    for other in range(send_ref.shape[0]):
        send_ref[other] = block


def arrived(got_ref, table_ref):
    return total(
        got_ref[part].astype(F32) * table_ref[part] for part in range(got_ref.shape[0])
    )


def first_kernel(
    starts_hbm, key_hbm, value_hbm, rate_hbm, send_ref, ends_ref, starts_ref, pair_ref, rate_ref, data_ref, sems
):
    tokens, width = key_hbm.shape
    tiles, groups = tokens // TILE, width // LANES
    me = lax.axis_index("seq")
    small = [
        pltpu.make_async_copy(rate_hbm, rate_ref, sems.at[2 * groups]),
        pltpu.make_async_copy(starts_hbm, starts_ref, sems.at[2 * groups + 1]),
    ]
    large = [
        [
            pltpu.make_async_copy(
                array.at[:, lane_group(group)], pair_ref.at[index, group], sems.at[2 * group + index]
            )
            for index, array in enumerate((key_hbm, value_hbm))
        ]
        for group in range(groups)
    ]
    for copy in large[0] + small + sum(large[1:], []):
        copy.start()
    for copy in large[0] + small:
        copy.wait()
    fulls = []
    for group in range(groups):
        if group:
            for copy in large[group]:
                copy.wait()
        rate = rate_ref[:, lane_group(group)]
        data_ref[group] = rounded(pair_ref[0, group].astype(F32) * pair_ref[1, group].astype(F32))
        factors = per_mode(jnp.exp(-rate), tiles)

        def step(offset, states):
            x = data_ref[group, pl.ds(offset, tiles, stride=TILE), :]
            return advance(factors, states, x)

        zero = jnp.zeros((tiles, LANES), F32)
        put_states(ends_ref, group, over_tile(step, (zero,) * MODES, False), tiles)
        tile_decay = jnp.exp(-rate * TILE)
        full = ends_ref[group, rows_of(0), :]
        for tile in range(1, tiles):
            alive = survive(starts_ref, me * tiles + tile)
            full = ends_ref[group, rows_of(tile), :] + tile_decay * alive * full
        fulls.append(full)
    send_state(fulls, send_ref)


def forward_local_kernel(
    starts_ref,
    key_ref,
    value_ref,
    query_ref,
    cot_ref,
    rate_ref,
    weight_ref,
    skip_ref,
    gain_ref,
    ends_ref,
    conv_ref,
    query_woven_ref,
    pull_ref,
    table_ref,
    data_ref,
    split_query_ref,
    split_pull_ref,
    enter_ref,
):
    tokens, width = key_ref.shape
    tiles, groups = tokens // TILE, width // LANES
    parts = table_ref.shape[0]
    me = lax.axis_index("seq")
    for group in range(groups):
        lanes = lane_group(group)
        rate = rate_ref[:, lanes]
        query = query_ref[:, lanes].astype(F32)
        data_ref[group] = rounded(key_ref[:, lanes].astype(F32) * value_ref[:, lanes].astype(F32))
        split_query_ref[group] = query
        split_pull_ref[group] = cot_ref[:, lanes].astype(F32) * gain_ref[:, lanes] * query
        tile_decay = jnp.exp(-rate * TILE)
        state = jnp.zeros((MODES, LANES), F32)
        for tile in range(tiles):
            enter = state * survive(starts_ref, me * tiles + tile)
            enter_ref[group, rows_of(tile), :] = enter
            state = ends_ref[group, rows_of(tile), :] + tile_decay * enter
        factors = per_mode(jnp.exp(-rate), tiles)
        weights = per_mode(weight_ref[:, lanes], tiles)
        skip = jnp.broadcast_to(skip_ref[:, lanes], (tiles, LANES))

        def step(offset, states):
            rows, here = pl.ds(offset, tiles, stride=TILE), woven(offset, tiles)
            x = data_ref[group, rows, :]
            states = advance(factors, states, x)
            conv_ref[group, here, :] = total(w * s for w, s in zip(weights, states)) + skip * x
            query_woven_ref[group, here, :] = split_query_ref[group, rows, :]
            pull_ref[group, here, :] = split_pull_ref[group, rows, :]
            return states

        over_tile(step, get_states(enter_ref, group, tiles), False)
    part_decay = [jnp.exp(-rate_ref[:, lane_group(group)] * tokens) for group in range(groups)]
    share = [jnp.zeros((MODES, LANES), F32)] * groups
    for part in range(parts - 1, -1, -1):
        kept = keeps(starts_ref, (part + 1) * tiles, tiles) if part < parts - 1 else 0.0
        for group in range(groups):
            share[group] = jnp.where(part == me - 1, 1.0, share[group] * part_decay[group] * kept)
            table_ref[part, rows_of(group), :] = share[group]


def token_sums(array):
    return [
        lax.dot_general(
            jnp.ones((8, LANES), F32),
            array[lane_group(block)],
            (((1,), (1,)), ((), ())),
            precision=HIGHEST,
            preferred_element_type=F32,
        )
        for block in range(array.shape[0] // LANES)
    ]


def forward_join_kernel(
    starts_ref,
    rate_ref,
    weight_ref,
    conv_ref,
    query_ref,
    pull_ref,
    table_ref,
    got_ref,
    mixer_ref,
    sums_ref,
    enter_ref,
    square_ref,
    inner_ref,
):
    groups, tokens, _ = conv_ref.shape
    tiles = tokens // TILE
    me = lax.axis_index("seq")
    incoming = arrived(got_ref, table_ref)
    for group in range(groups):
        lanes = lane_group(group)
        rate = rate_ref[:, lanes]
        tile_decay = jnp.exp(-rate * TILE)
        state = incoming[rows_of(group)] * weight_ref[:, lanes]
        for tile in range(tiles):
            state = state * survive(starts_ref, me * tiles + tile)
            enter_ref[group, rows_of(tile), :] = state
            state = state * tile_decay
        factors = per_mode(jnp.exp(-rate), tiles)

        def step(offset, states):
            here = woven(offset, tiles)
            states = tuple(f * s for f, s in zip(factors, states))
            mixer = rounded(conv_ref[group, here, :] + total(states))
            mixer_ref[group, here, :] = mixer
            gated = query_ref[group, here, :] * mixer
            square, inner = gated * gated, pull_ref[group, here, :] * mixer
            if group:
                square, inner = square + square_ref[here, :], inner + inner_ref[here, :]
            square_ref[here, :] = square
            inner_ref[here, :] = inner
            return states

        over_tile(step, get_states(enter_ref, group, tiles), False)
    rows = token_sums(square_ref[...]) + token_sums(inner_ref[...])
    row = lax.broadcasted_iota(jnp.int32, (8, LANES), 0)
    block = rows[0]
    for index in range(1, len(rows)):
        block = jnp.where(row == index, rows[index], block)
    for other in range(sums_ref.shape[0]):
        sums_ref[other] = block


def between_kernel(starts_ref, rate_ref, query_ref, mixer_ref, push_ref, natural_ref, table_ref):
    groups, tokens, _ = mixer_ref.shape
    tiles = tokens // TILE
    parts = table_ref.shape[0]
    me = lax.axis_index("seq")
    for group in range(groups):
        query = query_ref[group]
        push_ref[group] = query * query * mixer_ref[group]

        def step(block, carry):
            for tile in range(tiles):
                base = pl.multiple_of(tile * TILE + block * 16, 16)
                pair = [
                    mixer_ref[group, pl.ds((block * 16 + half * 8) * tiles + tile, 8, stride=tiles), :]
                    for half in range(2)
                ]
                natural_ref[pl.ds(base, 16), lane_group(group)] = jnp.concatenate(pair, axis=0).astype(BF16)
            return carry

        lax.fori_loop(0, TILE // 16, step, 0, unroll=True)
    part_decay = [jnp.exp(-rate_ref[:, lane_group(group)] * tokens) for group in range(groups)]
    share = [jnp.zeros((MODES, LANES), F32)] * groups
    for part in range(parts):
        alive = survive(starts_ref, part * tiles)
        kept = keeps(starts_ref, (part - 1) * tiles + 1, tiles - 1) if part else 0.0
        for group in range(groups):
            before = jnp.where(part == me + 1, 1.0, share[group] * part_decay[group] * kept)
            share[group] = before * alive
            table_ref[part, rows_of(group), :] = share[group]


def backward_kernel(
    starts_ref,
    rate_ref,
    sums_ref,
    pull_ref,
    push_ref,
    adjoint_ref,
    send_ref,
    fronts_ref,
    scale_ref,
    shift_ref,
):
    groups, tokens, _ = pull_ref.shape
    tiles, blocks = tokens // TILE, tokens // LANES
    me = lax.axis_index("seq")
    sums = total(sums_ref[other] for other in range(sums_ref.shape[0]))
    rinv = lax.rsqrt(sums / D + 1e-05)
    lean = jnp.concatenate([sums[blocks:], sums[:blocks]], axis=0)
    lean = rinv * rinv * rinv * lean / D
    rinv, lean = jnp.transpose(rinv), jnp.transpose(lean)
    for block in range(blocks):
        rows = lane_group(block)
        scale_ref[rows, :] = jnp.broadcast_to(rinv[:, block : block + 1], (LANES, LANES))
        shift_ref[rows, :] = jnp.broadcast_to(lean[:, block : block + 1], (LANES, LANES))
    fulls = []
    for group in range(groups):
        rate = rate_ref[:, lane_group(group)]
        factors = per_mode(jnp.exp(-rate), tiles)

        def step(offset, states):
            here = woven(offset, tiles)
            x = scale_ref[here, :] * pull_ref[group, here, :] - shift_ref[here, :] * push_ref[group, here, :]
            x = rounded(x)
            adjoint_ref[group, here, :] = x
            return advance(factors, states, x)

        zero = jnp.zeros((tiles, LANES), F32)
        put_states(fronts_ref, group, over_tile(step, (zero,) * MODES, True), tiles)
        tile_decay = jnp.exp(-rate * TILE)
        full = fronts_ref[group, rows_of(tiles - 1), :]
        for tile in range(tiles - 2, -1, -1):
            alive = survive(starts_ref, me * tiles + tile + 1)
            full = fronts_ref[group, rows_of(tile), :] + tile_decay * alive * full
        fulls.append(full)
    send_state(fulls, send_ref)


def backward_local_kernel(
    starts_ref,
    query_ref,
    cot_ref,
    mixer_ref,
    gain_ref,
    scale_ref,
    shift_ref,
    adjoint_ref,
    rate_ref,
    weight_ref,
    skip_ref,
    fronts_ref,
    mixed_ref,
    grad_query_ref,
    conv_ref,
    enter_ref,
):
    tokens, width = query_ref.shape
    tiles, groups = tokens // TILE, width // LANES
    me = lax.axis_index("seq")
    for group in range(groups):
        lanes = lane_group(group)
        rate = rate_ref[:, lanes]
        tile_decay = jnp.exp(-rate * TILE)
        state = jnp.zeros((MODES, LANES), F32)
        for tile in range(tiles - 1, -1, -1):
            enter_ref[group, rows_of(tile), :] = state
            state = fronts_ref[group, rows_of(tile), :] + tile_decay * state
            state = state * survive(starts_ref, me * tiles + tile)
        factors = per_mode(jnp.exp(-rate), tiles)
        weights = per_mode(weight_ref[:, lanes], tiles)
        skip = jnp.broadcast_to(skip_ref[:, lanes], (tiles, LANES))

        def step(offset, states):
            here = woven(offset, tiles)
            x = adjoint_ref[group, here, :]
            states = advance(factors, states, x)
            conv_ref[group, here, :] = total(w * s for w, s in zip(weights, states)) + skip * x
            return states

        over_tile(step, get_states(enter_ref, group, tiles), True)
    for tile in range(tiles):
        rows = slice(tile * TILE, (tile + 1) * TILE)
        back = pl.ds(tile, TILE, stride=tiles)
        scale, shift = scale_ref[back, :], shift_ref[back, :]
        for group in range(groups):
            lanes = lane_group(group)
            gain = gain_ref[:, lanes]
            mixer = mixer_ref[rows, lanes].astype(F32)
            gated = query_ref[rows, lanes].astype(F32) * mixer
            scaled = cot_ref[rows, lanes].astype(F32) * gain
            mixed_ref[rows, lanes] = (gated * scale * gain).astype(BF16)
            grad_query_ref[rows, lanes] = ((scale * scaled - gated * shift) * mixer).astype(BF16)


def backward_join_kernel(
    starts_ref,
    rate_ref,
    weight_ref,
    conv_ref,
    table_ref,
    key_ref,
    value_ref,
    got_ref,
    grad_key_ref,
    grad_value_ref,
    split_ref,
    enter_ref,
):
    tokens, width = key_ref.shape
    tiles, groups = tokens // TILE, width // LANES
    me = lax.axis_index("seq")
    incoming = arrived(got_ref, table_ref)
    for group in range(groups):
        lanes = lane_group(group)
        rate = rate_ref[:, lanes]
        tile_decay = jnp.exp(-rate * TILE)
        state = incoming[rows_of(group)] * weight_ref[:, lanes]
        for tile in range(tiles - 1, -1, -1):
            enter_ref[group, rows_of(tile), :] = state
            state = state * tile_decay * survive(starts_ref, me * tiles + tile)
        factors = per_mode(jnp.exp(-rate), tiles)

        def step(offset, states):
            states = tuple(f * s for f, s in zip(factors, states))
            split_ref[group, pl.ds(offset, tiles, stride=TILE), :] = rounded(
                conv_ref[group, woven(offset, tiles), :] + total(states)
            )
            return states

        over_tile(step, get_states(enter_ref, group, tiles), True)
        dproduct = split_ref[group]
        grad_key_ref[:, lanes] = (dproduct * value_ref[:, lanes].astype(F32)).astype(BF16)
        grad_value_ref[:, lanes] = (dproduct * key_ref[:, lanes].astype(F32)).astype(BF16)


def call(kernel, ins, outs, scratch, work, vmem=16):
    return pl.pallas_call(
        kernel,
        out_shape=[jax.ShapeDtypeStruct(shape, dtype) for shape, dtype in outs],
        in_specs=[pl.BlockSpec(memory_space=space) for _, space in ins],
        out_specs=[pl.BlockSpec(memory_space=pltpu.VMEM) for _ in outs],
        scratch_shapes=[
            pltpu.VMEM(shape, F32) if isinstance(shape, tuple) else shape for shape in scratch
        ],
        compiler_params=pltpu.CompilerParams(vmem_limit_bytes=vmem * 1024 * 1024),
        cost_estimate=pl.CostEstimate(flops=work, bytes_accessed=work // 8, transcendentals=0),
    )(*[array for array, _ in ins])


def on_device(
    query_feat,
    key_feat,
    value_feat,
    decay_rate,
    residues,
    skip_gain,
    norm_gain,
    doc_starts,
    cotangent,
):
    tokens, width = query_feat.shape
    parts, peers = lax.axis_size("seq"), lax.axis_size("chan")
    tiles, groups = tokens // TILE, width // LANES
    starts = (doc_starts, pltpu.SMEM)
    weight = residues * jnp.sqrt(-jnp.expm1(-2.0 * decay_rate))
    skip, gain = skip_gain[None], norm_gain[None]
    whole, split, states = (tokens, width), (groups, tokens, LANES), (groups, tiles * MODES, LANES)
    block, spread = (parts, groups * MODES, LANES), (tokens, LANES)
    work = tokens * width

    def vmem(*arrays):
        return [(array, pltpu.VMEM) for array in arrays]

    send, ends = call(
        first_kernel,
        [(array, pl.ANY) for array in (doc_starts, key_feat, value_feat, decay_rate)],
        [(block, SEND), (states, F32)],
        [
            pltpu.SMEM(doc_starts.shape, jnp.int32),
            pltpu.VMEM((2, groups, tokens, LANES), BF16),
            (MODES, width),
            split,
            pltpu.SemaphoreType.DMA((2 * groups + 2,)),
        ],
        work * 20,
        60,
    )
    got = lax.all_to_all(send, "seq", 0, 0)
    conv, query_woven, pull, table = call(
        forward_local_kernel,
        [starts]
        + vmem(key_feat, value_feat, query_feat, cotangent, decay_rate, weight, skip, gain, ends),
        [(split, F32), (split, F32), (split, F32), (block, F32)],
        [split, split, split, states],
        work * 50,
    )
    mixer, sums = call(
        forward_join_kernel,
        [starts] + vmem(decay_rate, weight, conv, query_woven, pull, table, got),
        [(split, F32), ((peers, 8, LANES), F32)],
        [states, spread, spread],
        work * 30,
    )
    sums = lax.all_to_all(sums, "chan", 0, 0)
    push, natural, table = call(
        between_kernel,
        [starts] + vmem(decay_rate, query_woven, mixer),
        [(split, F32), (whole, BF16), (block, F32)],
        [],
        work * 20,
    )
    adjoint, send, fronts, scale, shift = call(
        backward_kernel,
        [starts] + vmem(decay_rate, sums, pull, push),
        [(split, F32), (block, SEND), (states, F32), (spread, F32), (spread, F32)],
        [],
        work * 30,
    )
    got = lax.all_to_all(send, "seq", 0, 0)
    mixed, grad_query, conv = call(
        backward_local_kernel,
        [starts]
        + vmem(
            query_feat,
            cotangent,
            natural,
            gain,
            scale,
            shift,
            adjoint,
            decay_rate,
            weight,
            skip,
            fronts,
        ),
        [(whole, BF16), (whole, BF16), (split, F32)],
        [states],
        work * 50,
    )
    grad_key, grad_value = call(
        backward_join_kernel,
        [starts] + vmem(decay_rate, weight, conv, table, key_feat, value_feat, got),
        [(whole, BF16), (whole, BF16)],
        [split, states],
        work * 30,
    )
    return mixed, grad_query, grad_key, grad_value


def solution(mesh):
    both = P("seq", "chan")
    in_specs = (
        both,
        both,
        both,
        P(None, "chan"),
        P(None, "chan"),
        P("chan"),
        P("chan"),
        P(),
        both,
    )
    return jax.shard_map(
        on_device, mesh=mesh, in_specs=in_specs, out_specs=(both,) * 4, check_vma=False
    )
```

```python
import functools

import jax
import jax.numpy as jnp
from jax import lax
from jax.experimental import pallas as pl
from jax.experimental.pallas import tpu as pltpu
from jax.sharding import PartitionSpec as P


D = 8192
MODES = 8
TILE = 64
LANES = 128
ROWS = 8
PAIR = 2 * ROWS
PITCH = TILE + MODES

GROUP_ROWS = 24
GAIN, SKIP = 16, 17
F32 = jnp.float32
BF16 = jnp.bfloat16
HIGHEST = lax.Precision.HIGHEST
SEND = BF16
UNROLL = 16


def rounded(array):
    return array.astype(BF16).astype(F32)


def lane_group(group):
    return slice(group * LANES, (group + 1) * LANES)


def rows_of(tile):
    return slice(tile * MODES, (tile + 1) * MODES)


def survive(starts_ref, index):
    return (1 - starts_ref[index]).astype(F32)


def keeps(starts_ref, first, count):
    found = starts_ref[first]
    for step in range(1, count):
        found = found + starts_ref[first + step]
    return jnp.where(found == 0, 1.0, 0.0)


def total(parts):
    parts = list(parts)
    while len(parts) > 1:
        parts = [sum(parts[i : i + 2][1:], parts[i]) for i in range(0, len(parts), 2)]
    return parts[0]


def wide(table, m):
    return jnp.broadcast_to(table[m : m + 1], (ROWS, LANES))


def per_mode(table):
    return [wide(table, m) for m in range(MODES)]


def phase_powers(rate, first, sign):
    power = lax.broadcasted_iota(jnp.int32, (ROWS, LANES), 0).astype(F32) * sign + first
    return [jnp.exp(-wide(rate, m) * power) for m in range(MODES)]


def weighted(powers, table):
    return [p * wide(table, m) for m, p in enumerate(powers)]


def advance(factors, states, x):
    return tuple(f * s + x for f, s in zip(factors, states))


class Copies:
    def __init__(self, sems):
        self.sems, self.used = sems, 0

    def start(self, source, target):
        copy = pltpu.make_async_copy(source, target, self.sems.at[self.used])
        self.used += 1
        copy.start()
        return copy


def send_state(states, send_ref):
    block = jnp.concatenate(states, axis=0).astype(send_ref.dtype)
    for other in range(send_ref.shape[0]):
        send_ref[other] = block


def gather_phases(states, powers):
    return jnp.concatenate(
        [jnp.sum(s * p, axis=0, keepdims=True) for s, p in zip(states, powers)], axis=0
    )


def first_kernel(
    starts_hbm,
    key_hbm,
    value_hbm,
    rate_hbm,
    send_ref,
    starts_ref,
    key_ref,
    value_ref,
    rate_ref,
    sems,
):
    tokens, width = key_hbm.shape
    tiles, groups = tokens // TILE, width // LANES
    me = lax.axis_index("seq")
    copies = Copies(sems)
    large = []
    for group in range(groups):
        lanes = lane_group(group)
        large.append(
            [
                copies.start(key_hbm.at[:, lanes], key_ref.at[group]),
                copies.start(value_hbm.at[:, lanes], value_ref.at[group]),
            ]
        )
        if group == 0:
            small = [copies.start(rate_hbm, rate_ref), copies.start(starts_hbm, starts_ref)]
    for copy in small:
        copy.wait()
    fulls = []
    for first in range(0, groups, 2):
        pair = range(first, min(first + 2, groups))
        rates = [rate_ref[:, lane_group(group)] for group in pair]
        factors = [per_mode(jnp.exp(-rate * ROWS)) for rate in rates]
        for group in pair:
            for copy in large[group]:
                copy.wait()
        states = [(jnp.zeros((ROWS, LANES), F32),) * MODES for _ in pair]
        for tile in range(tiles):
            if tile:
                alive = survive(starts_ref, me * tiles + tile)
                states = [tuple(s * alive for s in state) for state in states]
            for step in range(0, TILE, PAIR):
                rows = slice(tile * TILE + step, tile * TILE + step + PAIR)
                for index, group in enumerate(pair):
                    x = rounded(key_ref[group, rows, :].astype(F32) * value_ref[group, rows, :].astype(F32))
                    states[index] = advance(factors[index], states[index], x[:ROWS])
                    states[index] = advance(factors[index], states[index], x[ROWS:])
        for rate, state in zip(rates, states):
            fulls.append(gather_phases(state, phase_powers(rate, ROWS - 1, -1)))
    send_state(fulls, send_ref)


def per_tile(table, tiles):
    return [jnp.broadcast_to(table[m : m + 1], (tiles, LANES)) for m in range(MODES)]


def over_tile(step, first, reverse):
    def body(index, carry):
        return step(TILE - 1 - index if reverse else index, carry)

    return lax.fori_loop(0, TILE, body, first, unroll=UNROLL)


def tile_rows(tile, count=TILE, first=0):
    return slice(tile * PITCH + first, tile * PITCH + first + count)


def put_tiles(ref, group, data):
    for tile in range(data.shape[0] // TILE):
        ref[group, tile_rows(tile), :] = data[tile * TILE : (tile + 1) * TILE]


def local_conv(me, starts_ref, rate, weight, skip, data_ref, work_ref, conv_ref, group, reverse):
    tiles = data_ref.shape[1] // PITCH
    factors, weights = per_tile(jnp.exp(-rate), tiles), per_tile(weight, tiles)
    skip = jnp.broadcast_to(skip, (tiles, LANES))

    def rows(offset):
        return pl.ds(offset, tiles, stride=PITCH)

    def leave(offset, states):
        return advance(factors, states, data_ref[group, rows(offset), :])

    ends = over_tile(leave, (jnp.zeros((tiles, LANES), F32),) * MODES, reverse)
    for m in range(MODES):
        work_ref[group, rows(TILE + m), :] = ends[m]
    tile_decay = jnp.exp(-rate * TILE)
    state = jnp.zeros((MODES, LANES), F32)
    for tile in reversed(range(tiles)) if reverse else range(tiles):
        alive = survive(starts_ref, me * tiles + tile)
        here = tile_rows(tile, MODES, TILE)
        end = work_ref[group, here, :]
        if reverse:
            work_ref[group, here, :] = state
            state = (end + tile_decay * state) * alive
        else:
            state = state * alive
            work_ref[group, here, :] = state
            state = end + tile_decay * state

    def step(offset, states):
        x = data_ref[group, rows(offset), :]
        states = advance(factors, states, x)
        work_ref[group, rows(offset), :] = total(w * s for w, s in zip(weights, states)) + skip * x
        return states

    over_tile(step, tuple(work_ref[group, rows(TILE + m), :] for m in range(MODES)), reverse)
    for tile in range(tiles):
        conv_ref[group, tile * TILE : (tile + 1) * TILE, :] = work_ref[group, tile_rows(tile), :]


def table_rows(tiles, groups, parts):
    return groups * GROUP_ROWS + tiles + parts


def put_flag(ref, row, value):
    ref[row : row + 1, :] = jnp.full((1, LANES), value)


def get_flag(ref, row):
    return jnp.broadcast_to(ref[row : row + 1, :], (ROWS, LANES))


class Table:
    def __init__(self, ref, tiles, groups):
        self.ref, self.groups = ref, groups
        self.flags = groups * GROUP_ROWS
        self.parts = self.flags + tiles

    def rows(self, group, first, count):
        first += group * GROUP_ROWS
        return slice(first, first + count)

    def rate(self, group):
        return self.ref[self.rows(group, 0, MODES), :]

    def weight(self, group):
        return self.ref[self.rows(group, MODES, MODES), :]

    def gain(self, group):
        return self.ref[self.rows(group, GAIN, 1), :]

    def skip(self, group):
        return self.ref[self.rows(group, SKIP, 1), :]

    def alive(self, tile):
        return get_flag(self.ref, self.flags + tile)

    def kept(self, part):
        return get_flag(self.ref, self.parts + part)


def forward_local_kernel(
    starts_ref,
    key_ref,
    value_ref,
    rate_ref,
    weight_ref,
    gain_ref,
    skip_ref,
    conv_ref,
    table_ref,
    data_ref,
    work_ref,
):
    tokens, width = key_ref.shape
    tiles, groups = tokens // TILE, width // LANES
    me = lax.axis_index("seq")
    table = Table(table_ref, tiles, groups)
    for group in range(groups):
        lanes = lane_group(group)
        put_tiles(data_ref, group, rounded(key_ref[:, lanes].astype(F32) * value_ref[:, lanes].astype(F32)))
        rate, weight, skip = rate_ref[:, lanes], weight_ref[:, lanes], skip_ref[:, lanes]
        local_conv(me, starts_ref, rate, weight, skip, data_ref, work_ref, conv_ref, group, False)
        table_ref[table.rows(group, 0, MODES), :] = rate
        table_ref[table.rows(group, MODES, MODES), :] = weight
        table_ref[table.rows(group, GAIN, 1), :] = gain_ref[:, lanes]
        table_ref[table.rows(group, SKIP, 1), :] = skip
    for tile in range(tiles):
        put_flag(table_ref, table.flags + tile, survive(starts_ref, me * tiles + tile))
    for part in range(starts_ref.shape[0] // tiles):
        put_flag(table_ref, table.parts + part, keeps(starts_ref, part * tiles, tiles))


def token_sums(array):
    return [
        lax.dot_general(
            jnp.ones((ROWS, LANES), F32),
            array[lane_group(block)],
            (((1,), (1,)), ((), ())),
            precision=HIGHEST,
            preferred_element_type=F32,
        )
        for block in range(array.shape[0] // LANES)
    ]


def part_of(got_ref, part, groups):
    return [got_ref[part, rows_of(group), :].astype(F32) for group in range(groups)]


def forward_join_kernel(
    table_ref,
    got_ref,
    conv_ref,
    query_ref,
    cot_ref,
    mixer_ref,
    sums_ref,
    square_ref,
    inner_ref,
):
    tokens, width = query_ref.shape
    tiles, groups = tokens // TILE, width // LANES
    table = Table(table_ref, tiles, groups)
    parts = got_ref.shape[0]
    me = lax.axis_index("seq")
    rates = [table.rate(group) for group in range(groups)]
    part_decay = [jnp.exp(-rate * tokens) for rate in rates]
    states = [jnp.zeros((MODES, LANES), F32)] * groups
    for part in range(parts - 1):
        kept = table.kept(part)
        arrived = part_of(got_ref, part, groups)
        states = [
            jnp.where(part < me, a + d * kept * s, s) for a, d, s in zip(arrived, part_decay, states)
        ]
    for group in range(groups):
        lanes = lane_group(group)
        factors = per_mode(jnp.exp(-rates[group] * ROWS))
        carry = weighted(phase_powers(rates[group], 1, 1), states[group] * table.weight(group))
        gain = jnp.broadcast_to(table.gain(group), (PAIR, LANES))
        for tile in range(tiles):
            alive = table.alive(tile)
            carry = [c * alive for c in carry]
            for step in range(0, TILE, PAIR):
                rows = slice(tile * TILE + step, tile * TILE + step + PAIR)
                extra = []
                for _ in range(2):
                    extra.append(total(carry))
                    carry = [c * f for c, f in zip(carry, factors)]
                mixer = (conv_ref[group, rows, :] + jnp.concatenate(extra, axis=0)).astype(BF16)
                mixer_ref[rows, lanes] = mixer
                gated = query_ref[rows, lanes].astype(F32) * mixer.astype(F32)
                square = gated * gated
                inner = cot_ref[rows, lanes].astype(F32) * gain * gated
                if group:
                    square, inner = square + square_ref[rows, :], inner + inner_ref[rows, :]
                square_ref[rows, :] = square
                inner_ref[rows, :] = inner
    sums = token_sums(square_ref[...]) + token_sums(inner_ref[...])
    row = lax.broadcasted_iota(jnp.int32, (ROWS, LANES), 0)
    block = sums[0]
    for index in range(1, len(sums)):
        block = jnp.where(row == index, sums[index], block)
    for other in range(sums_ref.shape[0]):
        sums_ref[other] = block


def spread_sums(sums, scale_ref, shift_ref):
    blocks = scale_ref.shape[0] // LANES
    rinv = lax.rsqrt(sums / D + 1e-05)
    lean = jnp.concatenate([sums[blocks:], sums[:blocks]], axis=0)
    lean = rinv * rinv * rinv * lean / D
    rinv, lean = jnp.transpose(rinv), jnp.transpose(lean)
    for block in range(blocks):
        rows = lane_group(block)
        scale_ref[rows, :] = jnp.broadcast_to(rinv[:, block : block + 1], (LANES, LANES))
        shift_ref[rows, :] = jnp.broadcast_to(lean[:, block : block + 1], (LANES, LANES))


def backward_kernel(
    table_ref,
    sums_ref,
    query_ref,
    cot_ref,
    mixer_ref,
    adjoint_ref,
    send_ref,
    totals_ref,
    scale_ref,
    shift_ref,
):
    tokens, width = query_ref.shape
    tiles, groups = tokens // TILE, width // LANES
    table = Table(table_ref, tiles, groups)
    sums = total(sums_ref[other] for other in range(sums_ref.shape[0]))
    totals_ref[...] = sums
    spread_sums(sums, scale_ref, shift_ref)
    fulls = []
    for group in range(groups):
        lanes = lane_group(group)
        rate = table.rate(group)
        factors = per_mode(jnp.exp(-rate * ROWS))
        powers = phase_powers(rate, 0, 1)
        gain = jnp.broadcast_to(table.gain(group), (PAIR, LANES))
        states = (jnp.zeros((ROWS, LANES), F32),) * MODES
        for tile in reversed(range(tiles)):
            if tile < tiles - 1:
                alive = table.alive(tile + 1)
                states = tuple(s * alive for s in states)
            for step in reversed(range(0, TILE, PAIR)):
                rows = slice(tile * TILE + step, tile * TILE + step + PAIR)
                query = query_ref[rows, lanes].astype(F32)
                gated = query * mixer_ref[rows, lanes].astype(F32)
                scaled = cot_ref[rows, lanes].astype(F32) * gain
                adjoint = ((scale_ref[rows, :] * scaled - gated * shift_ref[rows, :]) * query).astype(BF16)
                adjoint_ref[rows, lanes] = adjoint
                x = adjoint.astype(F32)
                states = advance(factors, states, x[ROWS:])
                states = advance(factors, states, x[:ROWS])
        fulls.append(gather_phases(states, powers))
    send_state(fulls, send_ref)


def outputs_kernel(
    table_ref, totals_ref, query_ref, cot_ref, mixer_ref, mixed_ref, grad_query_ref, done_ref, scale_ref, shift_ref
):
    tokens, width = query_ref.shape
    tiles, groups = tokens // TILE, width // LANES
    table = Table(table_ref, tiles, groups)
    spread_sums(totals_ref[...], scale_ref, shift_ref)
    for group in range(groups):
        lanes = lane_group(group)
        gain = jnp.broadcast_to(table.gain(group), (TILE, LANES))
        for tile in range(tiles):
            rows = slice(tile * TILE, (tile + 1) * TILE)
            scale, shift = scale_ref[rows, :], shift_ref[rows, :]
            mixer = mixer_ref[rows, lanes].astype(F32)
            gated = query_ref[rows, lanes].astype(F32) * mixer
            scaled = cot_ref[rows, lanes].astype(F32) * gain
            mixed_ref[rows, lanes] = (gated * scale * gain).astype(BF16)
            grad_query_ref[rows, lanes] = ((scale * scaled - gated * shift) * mixer).astype(BF16)
    done_ref[...] = totals_ref[...]


def backward_local_kernel(
    starts_ref, table_ref, adjoint_ref, done_ref, conv_ref, flags_ref, data_ref, work_ref
):
    tokens, width = adjoint_ref.shape
    tiles, groups = tokens // TILE, width // LANES
    me = lax.axis_index("seq")
    table = Table(table_ref, tiles, groups)
    for group in range(groups):
        put_tiles(data_ref, group, adjoint_ref[:, lane_group(group)].astype(F32))
        rate, weight, skip = table.rate(group), table.weight(group), table.skip(group)
        local_conv(me, starts_ref, rate, weight, skip, data_ref, work_ref, conv_ref, group, True)
    for part in range(starts_ref.shape[0] // tiles):
        put_flag(flags_ref, 2 * part, keeps(starts_ref, part * tiles + 1, tiles - 1))
        put_flag(flags_ref, 2 * part + 1, survive(starts_ref, part * tiles))


def backward_join_kernel(
    table_ref,
    flags_ref,
    got_ref,
    conv_ref,
    key_ref,
    value_ref,
    grad_key_hbm,
    grad_value_hbm,
    grad_key_ref,
    grad_value_ref,
    sems,
):
    tokens, width = key_ref.shape
    tiles, groups = tokens // TILE, width // LANES
    table = Table(table_ref, tiles, groups)
    parts = got_ref.shape[0]
    me = lax.axis_index("seq")
    copies = Copies(sems)
    rates = [table.rate(group) for group in range(groups)]
    part_decay = [jnp.exp(-rate * tokens) for rate in rates]
    states = [jnp.zeros((MODES, LANES), F32)] * groups
    for part in range(parts - 1, 0, -1):
        inner, alive = get_flag(flags_ref, 2 * part), get_flag(flags_ref, 2 * part + 1)
        arrived = part_of(got_ref, part, groups)
        states = [
            jnp.where(part > me, (a + d * inner * s) * alive, s)
            for a, d, s in zip(arrived, part_decay, states)
        ]
    out = []
    for group in range(groups):
        lanes = lane_group(group)
        factors = per_mode(jnp.exp(-rates[group] * ROWS))
        carry = weighted(phase_powers(rates[group], ROWS, -1), states[group] * table.weight(group))
        for tile in reversed(range(tiles)):
            if tile < tiles - 1:
                alive = table.alive(tile + 1)
                carry = [c * alive for c in carry]
            for step in reversed(range(0, TILE, PAIR)):
                rows = slice(tile * TILE + step, tile * TILE + step + PAIR)
                extra = []
                for _ in range(2):
                    extra.append(total(carry))
                    carry = [c * f for c, f in zip(carry, factors)]
                dproduct = rounded(conv_ref[group, rows, :] + jnp.concatenate(extra[::-1], axis=0))
                grad_key_ref[group, rows, :] = (dproduct * value_ref[rows, lanes].astype(F32)).astype(BF16)
                grad_value_ref[group, rows, :] = (dproduct * key_ref[rows, lanes].astype(F32)).astype(BF16)
        out.append(copies.start(grad_key_ref.at[group], grad_key_hbm.at[:, lanes]))
        out.append(copies.start(grad_value_ref.at[group], grad_value_hbm.at[:, lanes]))
    for copy in out:
        copy.wait()


def scratch_of(item):
    if isinstance(item, tuple):
        return pltpu.VMEM(*item) if isinstance(item[0], tuple) else pltpu.VMEM(item, F32)
    return item


def call(kernel, ins, outs, scratch, work, vmem=16):
    return pl.pallas_call(
        kernel,
        out_shape=[jax.ShapeDtypeStruct(*out[:2]) for out in outs],
        in_specs=[pl.BlockSpec(memory_space=space) for _, space in ins],
        out_specs=[pl.BlockSpec(memory_space=(*out, pltpu.VMEM)[2]) for out in outs],
        scratch_shapes=[scratch_of(item) for item in scratch],
        compiler_params=pltpu.CompilerParams(vmem_limit_bytes=vmem * 1024 * 1024),
        cost_estimate=pl.CostEstimate(flops=work, bytes_accessed=work // 8, transcendentals=0),
    )(*[array for array, _ in ins])


def on_device(
    query_feat,
    key_feat,
    value_feat,
    decay_rate,
    residues,
    skip_gain,
    norm_gain,
    doc_starts,
    cotangent,
):
    tokens, width = query_feat.shape
    parts, peers = lax.axis_size("seq"), lax.axis_size("chan")
    tiles, groups = tokens // TILE, width // LANES
    starts = (doc_starts, pltpu.SMEM)
    weight = residues * jnp.sqrt(-jnp.expm1(-2.0 * decay_rate))
    skip, gain = skip_gain[None], norm_gain[None]
    whole, split, pitched = (tokens, width), (groups, tokens, LANES), (groups, tiles * PITCH, LANES)
    block, spread, summed = (parts, groups * MODES, LANES), (tokens, LANES), (peers, ROWS, LANES)
    modes, packed = (MODES, width), (table_rows(tiles, groups, parts), LANES)
    work = tokens * width

    def vmem(*arrays):
        return [(array, pltpu.VMEM) for array in arrays]

    def hbm(*arrays):
        return [(array, pl.ANY) for array in arrays]

    def sems(count):
        return pltpu.SemaphoreType.DMA((count,))

    (send,) = call(
        first_kernel,
        hbm(doc_starts, key_feat, value_feat, decay_rate),
        [(block, SEND)],
        [
            pltpu.SMEM(doc_starts.shape, jnp.int32),
            (split, BF16),
            (split, BF16),
            modes,
            sems(2 * groups + 2),
        ],
        work * 20,
        60,
    )
    got = lax.all_to_all(send, "seq", 0, 0)
    conv, table = call(
        forward_local_kernel,
        [starts] + vmem(key_feat, value_feat, decay_rate, weight, gain, skip),
        [(split, F32), (packed, F32)],
        [pitched, pitched],
        work * 50,
    )
    mixer, sums = call(
        forward_join_kernel,
        vmem(table, got, conv, query_feat, cotangent),
        [(whole, BF16), (summed, F32)],
        [spread, spread],
        work * 30,
    )
    sums = lax.all_to_all(sums, "chan", 0, 0)
    adjoint, send, totals = call(
        backward_kernel,
        vmem(table, sums, query_feat, cotangent, mixer),
        [(whole, BF16), (block, SEND), ((ROWS, LANES), F32)],
        [spread, spread],
        work * 30,
    )
    got = lax.all_to_all(send, "seq", 0, 0)
    mixed, grad_query, done = call(
        outputs_kernel,
        vmem(table, totals, query_feat, cotangent, mixer),
        [(whole, BF16), (whole, BF16), ((ROWS, LANES), F32)],
        [spread, spread],
        work * 20,
    )
    conv, flags = call(
        backward_local_kernel,
        [starts] + vmem(table, adjoint, done),
        [(split, F32), ((2 * parts, LANES), F32)],
        [pitched, pitched],
        work * 50,
    )
    grad_key, grad_value = call(
        backward_join_kernel,
        vmem(table, flags, got, conv, key_feat, value_feat),
        [(whole, BF16, pl.ANY), (whole, BF16, pl.ANY)],
        [(split, BF16), (split, BF16), sems(2 * groups)],
        work * 30,
    )
    return mixed, grad_query, grad_key, grad_value


def solution(mesh):
    both = P("seq", "chan")
    in_specs = (
        both,
        both,
        both,
        P(None, "chan"),
        P(None, "chan"),
        P("chan"),
        P("chan"),
        P(),
        both,
    )
    return jax.shard_map(
        on_device, mesh=mesh, in_specs=in_specs, out_specs=(both,) * 4, check_vma=False
    )
```

```python
import functools

import jax
import jax.numpy as jnp
from jax import lax
from jax.experimental import pallas as pl
from jax.experimental.pallas import tpu as pltpu
from jax.sharding import PartitionSpec as P


D = 8192
MODES = 8
TILE = 64
LANES = 128
ROWS = 8
PAIR = 2 * ROWS
PITCH = TILE + MODES

GROUP_ROWS = 24
GAIN, SKIP = 16, 17
F32 = jnp.float32
BF16 = jnp.bfloat16
HIGHEST = lax.Precision.HIGHEST
SEND = BF16
UNROLL = 16
LAG = 1


def rounded(array):
    return array.astype(BF16).astype(F32)


def lane_group(group):
    return slice(group * LANES, (group + 1) * LANES)


def rows_of(tile):
    return slice(tile * MODES, (tile + 1) * MODES)


def survive(starts_ref, index):
    return (1 - starts_ref[index]).astype(F32)


def keeps(starts_ref, first, count):
    found = starts_ref[first]
    for step in range(1, count):
        found = found + starts_ref[first + step]
    return jnp.where(found == 0, 1.0, 0.0)


def total(parts):
    parts = list(parts)
    while len(parts) > 1:
        parts = [sum(parts[i : i + 2][1:], parts[i]) for i in range(0, len(parts), 2)]
    return parts[0]


def wide(table, m):
    return jnp.broadcast_to(table[m : m + 1], (ROWS, LANES))


def per_mode(table):
    return [wide(table, m) for m in range(MODES)]


def phase_powers(rate, first, sign):
    power = lax.broadcasted_iota(jnp.int32, (ROWS, LANES), 0).astype(F32) * sign + first
    return [jnp.exp(-wide(rate, m) * power) for m in range(MODES)]


def weighted(powers, table):
    return [p * wide(table, m) for m, p in enumerate(powers)]


def advance(factors, states, x):
    return tuple(f * s + x for f, s in zip(factors, states))


class Copies:
    def __init__(self, sems):
        self.sems, self.used = sems, 0

    def start(self, source, target):
        copy = pltpu.make_async_copy(source, target, self.sems.at[self.used])
        self.used += 1
        copy.start()
        return copy


def send_state(states, send_ref):
    block = jnp.concatenate(states, axis=0).astype(send_ref.dtype)
    for other in range(send_ref.shape[0]):
        send_ref[other] = block


def gather_phases(states, powers):
    return jnp.concatenate(
        [jnp.sum(s * p, axis=0, keepdims=True) for s, p in zip(states, powers)], axis=0
    )


def first_kernel(
    starts_hbm,
    key_hbm,
    value_hbm,
    rate_hbm,
    send_ref,
    starts_ref,
    key_ref,
    value_ref,
    rate_ref,
    sems,
):
    tokens, width = key_hbm.shape
    tiles, groups = tokens // TILE, width // LANES
    me = lax.axis_index("seq")
    copies = Copies(sems)
    large = []
    for group in range(groups):
        lanes = lane_group(group)
        large.append(
            [
                copies.start(key_hbm.at[:, lanes], key_ref.at[group]),
                copies.start(value_hbm.at[:, lanes], value_ref.at[group]),
            ]
        )
        if group == 0:
            small = [copies.start(rate_hbm, rate_ref), copies.start(starts_hbm, starts_ref)]
    for copy in small:
        copy.wait()
    fulls = []
    for group in range(groups):
        rate = rate_ref[:, lane_group(group)]
        factors = per_mode(jnp.exp(-rate * ROWS))
        powers = phase_powers(rate, ROWS - 1, -1)
        for copy in large[group]:
            copy.wait()
        states = (jnp.zeros((ROWS, LANES), F32),) * MODES
        for tile in range(tiles):
            if tile:
                alive = survive(starts_ref, me * tiles + tile)
                states = tuple(s * alive for s in states)
            for step in range(0, TILE, PAIR):
                rows = slice(tile * TILE + step, tile * TILE + step + PAIR)
                x = rounded(key_ref[group, rows, :].astype(F32) * value_ref[group, rows, :].astype(F32))
                states = advance(factors, states, x[:ROWS])
                states = advance(factors, states, x[ROWS:])
        fulls.append(gather_phases(states, powers))
    send_state(fulls, send_ref)


def per_tile(table, tiles):
    return [jnp.broadcast_to(table[m : m + 1], (tiles, LANES)) for m in range(MODES)]


def over_tile(step, first, reverse):
    def body(index, carry):
        return step(TILE - 1 - index if reverse else index, carry)

    return lax.fori_loop(0, TILE, body, first, unroll=UNROLL)


def tile_rows(tile, count=TILE, first=0):
    return slice(tile * PITCH + first, tile * PITCH + first + count)


def put_tiles(ref, group, data):
    for tile in range(data.shape[0] // TILE):
        ref[group, tile_rows(tile), :] = data[tile * TILE : (tile + 1) * TILE]


def local_conv(me, starts_ref, rate, weight, skip, data_ref, work_ref, conv_ref, group, reverse):
    tiles = data_ref.shape[1] // PITCH
    factors, weights = per_tile(jnp.exp(-rate), tiles), per_tile(weight, tiles)
    skip = jnp.broadcast_to(skip, (tiles, LANES))

    def rows(offset):
        return pl.ds(offset, tiles, stride=PITCH)

    def leave(offset, states):
        return advance(factors, states, data_ref[group, rows(offset), :])

    ends = over_tile(leave, (jnp.zeros((tiles, LANES), F32),) * MODES, reverse)
    for m in range(MODES):
        work_ref[group, rows(TILE + m), :] = ends[m]
    tile_decay = jnp.exp(-rate * TILE)
    state = jnp.zeros((MODES, LANES), F32)
    for tile in reversed(range(tiles)) if reverse else range(tiles):
        alive = survive(starts_ref, me * tiles + tile)
        here = tile_rows(tile, MODES, TILE)
        end = work_ref[group, here, :]
        if reverse:
            work_ref[group, here, :] = state
            state = (end + tile_decay * state) * alive
        else:
            state = state * alive
            work_ref[group, here, :] = state
            state = end + tile_decay * state

    def step(offset, states):
        x = data_ref[group, rows(offset), :]
        states = advance(factors, states, x)
        work_ref[group, rows(offset), :] = total(w * s for w, s in zip(weights, states)) + skip * x
        return states

    over_tile(step, tuple(work_ref[group, rows(TILE + m), :] for m in range(MODES)), reverse)
    for tile in range(tiles):
        conv_ref[group, tile * TILE : (tile + 1) * TILE, :] = work_ref[group, tile_rows(tile), :]


def table_rows(tiles, groups, parts):
    return groups * GROUP_ROWS + tiles + parts


def put_flag(ref, row, value):
    ref[row : row + 1, :] = jnp.full((1, LANES), value)


def get_flag(ref, row):
    return jnp.broadcast_to(ref[row : row + 1, :], (ROWS, LANES))


class Table:
    def __init__(self, ref, tiles, groups):
        self.ref, self.groups = ref, groups
        self.flags = groups * GROUP_ROWS
        self.parts = self.flags + tiles

    def rows(self, group, first, count):
        first += group * GROUP_ROWS
        return slice(first, first + count)

    def rate(self, group):
        return self.ref[self.rows(group, 0, MODES), :]

    def weight(self, group):
        return self.ref[self.rows(group, MODES, MODES), :]

    def gain(self, group):
        return self.ref[self.rows(group, GAIN, 1), :]

    def skip(self, group):
        return self.ref[self.rows(group, SKIP, 1), :]

    def alive(self, tile):
        return get_flag(self.ref, self.flags + tile)

    def kept(self, part):
        return get_flag(self.ref, self.parts + part)


def forward_local_kernel(
    starts_ref,
    key_ref,
    value_ref,
    rate_ref,
    weight_ref,
    gain_ref,
    skip_ref,
    conv_ref,
    table_ref,
    data_ref,
    work_ref,
):
    tokens, width = key_ref.shape
    tiles, groups = tokens // TILE, width // LANES
    me = lax.axis_index("seq")
    table = Table(table_ref, tiles, groups)
    for group in range(groups):
        lanes = lane_group(group)
        put_tiles(data_ref, group, rounded(key_ref[:, lanes].astype(F32) * value_ref[:, lanes].astype(F32)))
        rate, weight, skip = rate_ref[:, lanes], weight_ref[:, lanes], skip_ref[:, lanes]
        local_conv(me, starts_ref, rate, weight, skip, data_ref, work_ref, conv_ref, group, False)
        table_ref[table.rows(group, 0, MODES), :] = rate
        table_ref[table.rows(group, MODES, MODES), :] = weight
        table_ref[table.rows(group, GAIN, 1), :] = gain_ref[:, lanes]
        table_ref[table.rows(group, SKIP, 1), :] = skip
    for tile in range(tiles):
        put_flag(table_ref, table.flags + tile, survive(starts_ref, me * tiles + tile))
    for part in range(starts_ref.shape[0] // tiles):
        put_flag(table_ref, table.parts + part, keeps(starts_ref, part * tiles, tiles))


def token_sums(array):
    return [
        lax.dot_general(
            jnp.ones((ROWS, LANES), F32),
            array[lane_group(block)],
            (((1,), (1,)), ((), ())),
            precision=HIGHEST,
            preferred_element_type=F32,
        )
        for block in range(array.shape[0] // LANES)
    ]


def part_of(got_ref, part, groups):
    return [got_ref[part, rows_of(group), :].astype(F32) for group in range(groups)]


def forward_join_kernel(
    table_ref,
    got_ref,
    conv_ref,
    query_ref,
    cot_ref,
    mixer_ref,
    sums_ref,
    square_ref,
    inner_ref,
):
    tokens, width = query_ref.shape
    tiles, groups = tokens // TILE, width // LANES
    table = Table(table_ref, tiles, groups)
    parts = got_ref.shape[0]
    me = lax.axis_index("seq")
    rates = [table.rate(group) for group in range(groups)]
    part_decay = [jnp.exp(-rate * tokens) for rate in rates]
    states = [jnp.zeros((MODES, LANES), F32)] * groups
    for part in range(parts - 1):
        kept = table.kept(part)
        arrived = part_of(got_ref, part, groups)
        states = [
            jnp.where(part < me, a + d * kept * s, s) for a, d, s in zip(arrived, part_decay, states)
        ]
    for group in range(groups):
        lanes = lane_group(group)
        factors = per_mode(jnp.exp(-rates[group] * ROWS))
        carry = weighted(phase_powers(rates[group], 1, 1), states[group] * table.weight(group))
        gain = jnp.broadcast_to(table.gain(group), (PAIR, LANES))
        for tile in range(tiles):
            alive = table.alive(tile)
            carry = [c * alive for c in carry]
            for step in range(0, TILE, PAIR):
                rows = slice(tile * TILE + step, tile * TILE + step + PAIR)
                extra = []
                for _ in range(2):
                    extra.append(total(carry))
                    carry = [c * f for c, f in zip(carry, factors)]
                mixer = (conv_ref[group, rows, :] + jnp.concatenate(extra, axis=0)).astype(BF16)
                mixer_ref[rows, lanes] = mixer
                gated = query_ref[rows, lanes].astype(F32) * mixer.astype(F32)
                square = gated * gated
                inner = cot_ref[rows, lanes].astype(F32) * gain * gated
                if group:
                    square, inner = square + square_ref[rows, :], inner + inner_ref[rows, :]
                square_ref[rows, :] = square
                inner_ref[rows, :] = inner
    sums = token_sums(square_ref[...]) + token_sums(inner_ref[...])
    row = lax.broadcasted_iota(jnp.int32, (ROWS, LANES), 0)
    block = sums[0]
    for index in range(1, len(sums)):
        block = jnp.where(row == index, sums[index], block)
    for other in range(sums_ref.shape[0]):
        sums_ref[other] = block


def spread_sums(sums, scale_ref, shift_ref):
    blocks = scale_ref.shape[0] // LANES
    rinv = lax.rsqrt(sums / D + 1e-05)
    lean = jnp.concatenate([sums[blocks:], sums[:blocks]], axis=0)
    lean = rinv * rinv * rinv * lean / D
    rinv, lean = jnp.transpose(rinv), jnp.transpose(lean)
    for block in range(blocks):
        rows = lane_group(block)
        scale_ref[rows, :] = jnp.broadcast_to(rinv[:, block : block + 1], (LANES, LANES))
        shift_ref[rows, :] = jnp.broadcast_to(lean[:, block : block + 1], (LANES, LANES))


def backward_kernel(
    table_ref,
    sums_ref,
    query_ref,
    cot_ref,
    mixer_ref,
    adjoint_ref,
    send_ref,
    totals_ref,
    scale_ref,
    shift_ref,
):
    tokens, width = query_ref.shape
    tiles, groups = tokens // TILE, width // LANES
    table = Table(table_ref, tiles, groups)
    sums = total(sums_ref[other] for other in range(sums_ref.shape[0]))
    totals_ref[...] = sums
    spread_sums(sums, scale_ref, shift_ref)
    fulls = []
    for group in range(groups):
        lanes = lane_group(group)
        rate = table.rate(group)
        factors = per_mode(jnp.exp(-rate * ROWS))
        powers = phase_powers(rate, 0, 1)
        gain = jnp.broadcast_to(table.gain(group), (PAIR, LANES))
        states = (jnp.zeros((ROWS, LANES), F32),) * MODES
        for tile in reversed(range(tiles)):
            if tile < tiles - 1:
                alive = table.alive(tile + 1)
                states = tuple(s * alive for s in states)
            for step in reversed(range(0, TILE, PAIR)):
                rows = slice(tile * TILE + step, tile * TILE + step + PAIR)
                query = query_ref[rows, lanes].astype(F32)
                gated = query * mixer_ref[rows, lanes].astype(F32)
                scaled = cot_ref[rows, lanes].astype(F32) * gain
                adjoint = ((scale_ref[rows, :] * scaled - gated * shift_ref[rows, :]) * query).astype(BF16)
                adjoint_ref[rows, lanes] = adjoint
                x = adjoint.astype(F32)
                states = advance(factors, states, x[ROWS:])
                states = advance(factors, states, x[:ROWS])
        fulls.append(gather_phases(states, powers))
    send_state(fulls, send_ref)


def outputs_kernel(
    table_ref, totals_ref, query_ref, cot_ref, mixer_ref, mixed_ref, grad_query_ref, done_ref, scale_ref, shift_ref
):
    tokens, width = query_ref.shape
    tiles, groups = tokens // TILE, width // LANES
    table = Table(table_ref, tiles, groups)
    spread_sums(totals_ref[...], scale_ref, shift_ref)
    for group in range(groups):
        lanes = lane_group(group)
        gain = jnp.broadcast_to(table.gain(group), (TILE, LANES))
        for tile in range(tiles):
            rows = slice(tile * TILE, (tile + 1) * TILE)
            scale, shift = scale_ref[rows, :], shift_ref[rows, :]
            mixer = mixer_ref[rows, lanes].astype(F32)
            gated = query_ref[rows, lanes].astype(F32) * mixer
            scaled = cot_ref[rows, lanes].astype(F32) * gain
            mixed_ref[rows, lanes] = (gated * scale * gain).astype(BF16)
            grad_query_ref[rows, lanes] = ((scale * scaled - gated * shift) * mixer).astype(BF16)
    done_ref[...] = totals_ref[...]


def backward_local_kernel(
    starts_ref, table_ref, adjoint_ref, done_ref, conv_ref, flags_ref, data_ref, work_ref
):
    tokens, width = adjoint_ref.shape
    tiles, groups = tokens // TILE, width // LANES
    me = lax.axis_index("seq")
    table = Table(table_ref, tiles, groups)
    for group in range(groups):
        put_tiles(data_ref, group, adjoint_ref[:, lane_group(group)].astype(F32))
        rate, weight, skip = table.rate(group), table.weight(group), table.skip(group)
        local_conv(me, starts_ref, rate, weight, skip, data_ref, work_ref, conv_ref, group, True)
    for part in range(starts_ref.shape[0] // tiles):
        put_flag(flags_ref, 2 * part, keeps(starts_ref, part * tiles + 1, tiles - 1))
        put_flag(flags_ref, 2 * part + 1, survive(starts_ref, part * tiles))


def backward_join_kernel(
    table_ref,
    flags_ref,
    got_ref,
    conv_hbm,
    key_hbm,
    value_hbm,
    grad_key_hbm,
    grad_value_hbm,
    conv_ref,
    key_ref,
    value_ref,
    dproduct_ref,
    grad_key_ref,
    grad_value_ref,
    sems,
):
    tokens, width = key_hbm.shape
    tiles, groups = tokens // TILE, width // LANES
    table = Table(table_ref, tiles, groups)
    parts = got_ref.shape[0]
    me = lax.axis_index("seq")
    copies = Copies(sems)
    near = [copies.start(conv_hbm.at[group], conv_ref.at[group]) for group in range(groups)]
    large = []
    for group in range(groups):
        lanes = lane_group(group)
        large.append(
            [
                copies.start(value_hbm.at[:, lanes], value_ref.at[group]),
                copies.start(key_hbm.at[:, lanes], key_ref.at[group]),
            ]
        )
    rates = [table.rate(group) for group in range(groups)]
    part_decay = [jnp.exp(-rate * tokens) for rate in rates]
    states = [jnp.zeros((MODES, LANES), F32)] * groups
    for part in range(parts - 1, 0, -1):
        inner, alive = get_flag(flags_ref, 2 * part), get_flag(flags_ref, 2 * part + 1)
        arrived = part_of(got_ref, part, groups)
        states = [
            jnp.where(part > me, (a + d * inner * s) * alive, s)
            for a, d, s in zip(arrived, part_decay, states)
        ]
    out = []

    def finish(group):
        lanes = lane_group(group)
        for copy in large[group]:
            copy.wait()
        dproduct = dproduct_ref[group].astype(F32)
        grad_key_ref[group] = (dproduct * value_ref[group].astype(F32)).astype(BF16)
        out.append(copies.start(grad_key_ref.at[group], grad_key_hbm.at[:, lanes]))
        grad_value_ref[group] = (dproduct * key_ref[group].astype(F32)).astype(BF16)
        out.append(copies.start(grad_value_ref.at[group], grad_value_hbm.at[:, lanes]))

    for group in range(groups):
        lanes = lane_group(group)
        factors = per_mode(jnp.exp(-rates[group] * ROWS))
        carry = weighted(phase_powers(rates[group], ROWS, -1), states[group] * table.weight(group))
        near[group].wait()
        for tile in reversed(range(tiles)):
            if tile < tiles - 1:
                alive = table.alive(tile + 1)
                carry = [c * alive for c in carry]
            for step in reversed(range(0, TILE, PAIR)):
                rows = slice(tile * TILE + step, tile * TILE + step + PAIR)
                extra = []
                for _ in range(2):
                    extra.append(total(carry))
                    carry = [c * f for c, f in zip(carry, factors)]
                dproduct = conv_ref[group, rows, :] + jnp.concatenate(extra[::-1], axis=0)
                dproduct_ref[group, rows, :] = dproduct.astype(BF16)
        if group >= LAG:
            finish(group - LAG)
    for group in range(groups - LAG, groups):
        finish(group)
    for copy in out:
        copy.wait()


def scratch_of(item):
    if isinstance(item, tuple):
        return pltpu.VMEM(*item) if isinstance(item[0], tuple) else pltpu.VMEM(item, F32)
    return item


def call(kernel, ins, outs, scratch, work, vmem=16):
    return pl.pallas_call(
        kernel,
        out_shape=[jax.ShapeDtypeStruct(*out[:2]) for out in outs],
        in_specs=[pl.BlockSpec(memory_space=space) for _, space in ins],
        out_specs=[pl.BlockSpec(memory_space=(*out, pltpu.VMEM)[2]) for out in outs],
        scratch_shapes=[scratch_of(item) for item in scratch],
        compiler_params=pltpu.CompilerParams(vmem_limit_bytes=vmem * 1024 * 1024),
        cost_estimate=pl.CostEstimate(flops=work, bytes_accessed=work // 8, transcendentals=0),
    )(*[array for array, _ in ins])


def on_device(
    query_feat,
    key_feat,
    value_feat,
    decay_rate,
    residues,
    skip_gain,
    norm_gain,
    doc_starts,
    cotangent,
):
    tokens, width = query_feat.shape
    parts, peers = lax.axis_size("seq"), lax.axis_size("chan")
    tiles, groups = tokens // TILE, width // LANES
    starts = (doc_starts, pltpu.SMEM)
    weight = residues * jnp.sqrt(-jnp.expm1(-2.0 * decay_rate))
    skip, gain = skip_gain[None], norm_gain[None]
    whole, split, pitched = (tokens, width), (groups, tokens, LANES), (groups, tiles * PITCH, LANES)
    block, spread, summed = (parts, groups * MODES, LANES), (tokens, LANES), (peers, ROWS, LANES)
    modes, packed = (MODES, width), (table_rows(tiles, groups, parts), LANES)
    work = tokens * width

    def vmem(*arrays):
        return [(array, pltpu.VMEM) for array in arrays]

    def hbm(*arrays):
        return [(array, pl.ANY) for array in arrays]

    def sems(count):
        return pltpu.SemaphoreType.DMA((count,))

    (send,) = call(
        first_kernel,
        hbm(doc_starts, key_feat, value_feat, decay_rate),
        [(block, SEND)],
        [
            pltpu.SMEM(doc_starts.shape, jnp.int32),
            (split, BF16),
            (split, BF16),
            modes,
            sems(2 * groups + 2),
        ],
        work * 20,
        60,
    )
    got = lax.all_to_all(send, "seq", 0, 0)
    conv, table = call(
        forward_local_kernel,
        [starts] + vmem(key_feat, value_feat, decay_rate, weight, gain, skip),
        [(split, F32), (packed, F32)],
        [pitched, pitched],
        work * 50,
    )
    mixer, sums = call(
        forward_join_kernel,
        vmem(table, got, conv, query_feat, cotangent),
        [(whole, BF16), (summed, F32)],
        [spread, spread],
        work * 30,
    )
    sums = lax.all_to_all(sums, "chan", 0, 0)
    adjoint, send, totals = call(
        backward_kernel,
        vmem(table, sums, query_feat, cotangent, mixer),
        [(whole, BF16), (block, SEND), ((ROWS, LANES), F32)],
        [spread, spread],
        work * 30,
    )
    got = lax.all_to_all(send, "seq", 0, 0)
    mixed, grad_query, done = call(
        outputs_kernel,
        vmem(table, totals, query_feat, cotangent, mixer),
        [(whole, BF16), (whole, BF16), ((ROWS, LANES), F32)],
        [spread, spread],
        work * 20,
    )
    conv, flags = call(
        backward_local_kernel,
        [starts] + vmem(table, adjoint, done),
        [(split, F32), ((2 * parts, LANES), F32)],
        [pitched, pitched],
        work * 50,
    )
    grad_key, grad_value = call(
        backward_join_kernel,
        vmem(table, flags, got) + hbm(conv, key_feat, value_feat),
        [(whole, BF16, pl.ANY), (whole, BF16, pl.ANY)],
        [split] + [(split, BF16)] * 5 + [sems(5 * groups)],
        work * 30,
        53,
    )
    return mixed, grad_query, grad_key, grad_value


def solution(mesh):
    both = P("seq", "chan")
    in_specs = (
        both,
        both,
        both,
        P(None, "chan"),
        P(None, "chan"),
        P("chan"),
        P("chan"),
        P(),
        both,
    )
    return jax.shard_map(
        on_device, mesh=mesh, in_specs=in_specs, out_specs=(both,) * 4, check_vma=False
    )
```

```python
import functools

import jax
import jax.numpy as jnp
from jax import lax
from jax.experimental import pallas as pl
from jax.experimental.pallas import tpu as pltpu
from jax.sharding import PartitionSpec as P


D = 8192
MODES = 8
TILE = 64
LANES = 128
ROWS = 8
PAIR = 2 * ROWS
PITCH = TILE + MODES

GROUP_ROWS = 24
GAIN, SKIP = 16, 17
F32 = jnp.float32
BF16 = jnp.bfloat16
SEND = BF16
UNROLL = 16
LAG = 1
HEAD = 2


def rounded(array):
    return array.astype(BF16).astype(F32)


def lane_group(group):
    return slice(group * LANES, (group + 1) * LANES)


def rows_of(tile):
    return slice(tile * MODES, (tile + 1) * MODES)


def survive(starts_ref, index):
    return (1 - starts_ref[index]).astype(F32)


def keeps(starts_ref, first, count):
    found = starts_ref[first]
    for step in range(1, count):
        found = found + starts_ref[first + step]
    return jnp.where(found == 0, 1.0, 0.0)


def total(parts):
    parts = list(parts)
    while len(parts) > 1:
        parts = [sum(parts[i : i + 2][1:], parts[i]) for i in range(0, len(parts), 2)]
    return parts[0]


def wide(table, m):
    return jnp.broadcast_to(table[m : m + 1], (ROWS, LANES))


def per_mode(table):
    return [wide(table, m) for m in range(MODES)]


def phase_powers(rate, first, sign):
    power = lax.broadcasted_iota(jnp.int32, (ROWS, LANES), 0).astype(F32) * sign + first
    return [jnp.exp(-wide(rate, m) * power) for m in range(MODES)]


def weighted(powers, table):
    return [p * wide(table, m) for m, p in enumerate(powers)]


def advance(factors, states, x):
    return tuple(f * s + x for f, s in zip(factors, states))


class Copies:
    def __init__(self, sems):
        self.sems, self.used = sems, 0

    def start(self, source, target):
        copy = pltpu.make_async_copy(source, target, self.sems.at[self.used])
        self.used += 1
        copy.start()
        return copy


def send_state(states, send_ref):
    block = jnp.concatenate(states, axis=0).astype(send_ref.dtype)
    for other in range(send_ref.shape[0]):
        send_ref[other] = block


def gather_phases(states, powers):
    return jnp.concatenate(
        [jnp.sum(s * p, axis=0, keepdims=True) for s, p in zip(states, powers)], axis=0
    )


def first_kernel(
    starts_hbm,
    key_hbm,
    value_hbm,
    rate_hbm,
    send_ref,
    starts_ref,
    key_ref,
    value_ref,
    rate_ref,
    sems,
):
    tokens, width = key_hbm.shape
    tiles, groups = tokens // TILE, width // LANES
    me = lax.axis_index("seq")
    copies = Copies(sems)
    large = []
    for group in range(groups):
        lanes = lane_group(group)
        large.append(
            [
                copies.start(key_hbm.at[:, lanes], key_ref.at[group]),
                copies.start(value_hbm.at[:, lanes], value_ref.at[group]),
            ]
        )
        if group == 0:
            small = [copies.start(rate_hbm, rate_ref), copies.start(starts_hbm, starts_ref)]
    for copy in small:
        copy.wait()
    fulls = []
    for group in range(groups):
        rate = rate_ref[:, lane_group(group)]
        factors = per_mode(jnp.exp(-rate * ROWS))
        powers = phase_powers(rate, ROWS - 1, -1)
        for copy in large[group]:
            copy.wait()
        states = (jnp.zeros((ROWS, LANES), F32),) * MODES
        for tile in range(tiles):
            if tile:
                alive = survive(starts_ref, me * tiles + tile)
                states = tuple(s * alive for s in states)
            for step in range(0, TILE, PAIR):
                rows = slice(tile * TILE + step, tile * TILE + step + PAIR)
                x = (key_ref[group, rows, :] * value_ref[group, rows, :]).astype(F32)
                states = advance(factors, states, x[:ROWS])
                states = advance(factors, states, x[ROWS:])
        fulls.append(gather_phases(states, powers))
    send_state(fulls, send_ref)


def per_tile(table, tiles):
    return [jnp.broadcast_to(table[m : m + 1], (tiles, LANES)) for m in range(MODES)]


def over_tile(step, first, reverse):
    def body(index, carry):
        return step(TILE - 1 - index if reverse else index, carry)

    return lax.fori_loop(0, TILE, body, first, unroll=UNROLL)


def tile_rows(tile, count=TILE, first=0):
    return slice(tile * PITCH + first, tile * PITCH + first + count)


def put_tiles(ref, group, data):
    for tile in range(data.shape[0] // TILE):
        ref[group, tile_rows(tile), :] = data[tile * TILE : (tile + 1) * TILE]


def local_conv(me, starts_ref, rate, weight, skip, data_ref, work_ref, conv_ref, group, reverse):
    tiles = data_ref.shape[1] // PITCH
    factors, weights = per_tile(jnp.exp(-rate), tiles), per_tile(weight, tiles)
    skip = jnp.broadcast_to(skip, (tiles, LANES))

    def rows(offset):
        return pl.ds(offset, tiles, stride=PITCH)

    def leave(offset, states):
        return advance(factors, states, data_ref[group, rows(offset), :])

    ends = over_tile(leave, (jnp.zeros((tiles, LANES), F32),) * MODES, reverse)
    for m in range(MODES):
        work_ref[group, rows(TILE + m), :] = ends[m]
    tile_decay = jnp.exp(-rate * TILE)
    state = jnp.zeros((MODES, LANES), F32)
    for tile in reversed(range(tiles)) if reverse else range(tiles):
        alive = survive(starts_ref, me * tiles + tile)
        here = tile_rows(tile, MODES, TILE)
        end = work_ref[group, here, :]
        if reverse:
            work_ref[group, here, :] = state
            state = (end + tile_decay * state) * alive
        else:
            state = state * alive
            work_ref[group, here, :] = state
            state = end + tile_decay * state

    def step(offset, states):
        x = data_ref[group, rows(offset), :]
        states = advance(factors, states, x)
        work_ref[group, rows(offset), :] = total(w * s for w, s in zip(weights, states)) + skip * x
        return states

    over_tile(step, tuple(work_ref[group, rows(TILE + m), :] for m in range(MODES)), reverse)
    for tile in range(tiles):
        conv_ref[tile * TILE : (tile + 1) * TILE, :] = work_ref[group, tile_rows(tile), :]


def table_rows(tiles, groups, parts):
    return groups * GROUP_ROWS + tiles + parts


def put_flag(ref, row, value):
    ref[row : row + 1, :] = jnp.full((1, LANES), value)


def get_flag(ref, row):
    return jnp.broadcast_to(ref[row : row + 1, :], (ROWS, LANES))


class Table:
    def __init__(self, ref, tiles, groups):
        self.ref, self.groups = ref, groups
        self.flags = groups * GROUP_ROWS
        self.parts = self.flags + tiles

    def rows(self, group, first, count):
        first += group * GROUP_ROWS
        return slice(first, first + count)

    def rate(self, group):
        return self.ref[self.rows(group, 0, MODES), :]

    def weight(self, group):
        return self.ref[self.rows(group, MODES, MODES), :]

    def gain(self, group):
        return self.ref[self.rows(group, GAIN, 1), :]

    def skip(self, group):
        return self.ref[self.rows(group, SKIP, 1), :]

    def alive(self, tile):
        return get_flag(self.ref, self.flags + tile)

    def kept(self, part):
        return get_flag(self.ref, self.parts + part)


def forward_local_kernel(
    starts_ref,
    key_ref,
    value_ref,
    rate_ref,
    weight_ref,
    gain_ref,
    skip_ref,
    conv_ref,
    table_ref,
    data_ref,
    work_ref,
):
    tokens, width = key_ref.shape
    tiles, groups = tokens // TILE, width // LANES
    me = lax.axis_index("seq")
    table = Table(table_ref, tiles, groups)
    for group in range(groups):
        lanes = lane_group(group)
        put_tiles(data_ref, group, rounded(key_ref[:, lanes].astype(F32) * value_ref[:, lanes].astype(F32)))
        rate, weight, skip = rate_ref[:, lanes], weight_ref[:, lanes], skip_ref[:, lanes]
        local_conv(me, starts_ref, rate, weight, skip, data_ref, work_ref, conv_ref.at[group], group, False)
        table_ref[table.rows(group, 0, MODES), :] = rate
        table_ref[table.rows(group, MODES, MODES), :] = weight
        table_ref[table.rows(group, GAIN, 1), :] = gain_ref[:, lanes]
        table_ref[table.rows(group, SKIP, 1), :] = skip
    for tile in range(tiles):
        put_flag(table_ref, table.flags + tile, survive(starts_ref, me * tiles + tile))
    for part in range(starts_ref.shape[0] // tiles):
        put_flag(table_ref, table.parts + part, keeps(starts_ref, part * tiles, tiles))


def put_sums(sums, lane, array):
    lanes = lax.broadcasted_iota(jnp.int32, (ROWS, LANES), 1)
    return jnp.where(lanes == lane, jnp.sum(array, axis=1, keepdims=True), sums)


def part_of(got_ref, part, groups):
    return [got_ref[part, rows_of(group), :].astype(F32) for group in range(groups)]


def forward_join_kernel(
    table_ref,
    got_ref,
    conv_ref,
    query_ref,
    cot_ref,
    mixer_ref,
    sums_ref,
    square_ref,
    inner_ref,
):
    tokens, width = query_ref.shape
    tiles, groups = tokens // TILE, width // LANES
    table = Table(table_ref, tiles, groups)
    parts = got_ref.shape[0]
    me = lax.axis_index("seq")
    rates = [table.rate(group) for group in range(groups)]
    sums = jnp.zeros((ROWS, LANES), F32)
    part_decay = [jnp.exp(-rate * tokens) for rate in rates]
    states = [jnp.zeros((MODES, LANES), F32)] * groups
    for part in range(parts - 1):
        kept = table.kept(part)
        arrived = part_of(got_ref, part, groups)
        states = [
            jnp.where(part < me, a + d * kept * s, s) for a, d, s in zip(arrived, part_decay, states)
        ]
    for group in range(groups):
        lanes = lane_group(group)
        factors = per_mode(jnp.exp(-rates[group] * ROWS))
        carry = weighted(phase_powers(rates[group], 1, 1), states[group] * table.weight(group))
        gain = jnp.broadcast_to(table.gain(group), (PAIR, LANES))
        for tile in range(tiles):
            alive = table.alive(tile)
            carry = [c * alive for c in carry]
            for step in range(0, TILE, PAIR):
                rows = slice(tile * TILE + step, tile * TILE + step + PAIR)
                extra = []
                for _ in range(2):
                    extra.append(total(carry))
                    carry = [c * f for c, f in zip(carry, factors)]
                mixer = (conv_ref[group, rows, :] + jnp.concatenate(extra, axis=0)).astype(BF16)
                mixer_ref[rows, lanes] = mixer
                gated = query_ref[rows, lanes].astype(F32) * mixer.astype(F32)
                square = gated * gated
                inner = cot_ref[rows, lanes].astype(F32) * gain * gated
                if group:
                    square, inner = square + square_ref[rows, :], inner + inner_ref[rows, :]
                if group < groups - 1:
                    square_ref[rows, :] = square
                    inner_ref[rows, :] = inner
                    continue
                for half in range(2):
                    lane, part = (tile * TILE + step) // ROWS + half, slice(half * ROWS, (half + 1) * ROWS)
                    sums = put_sums(sums, lane, square[part])
                    sums = put_sums(sums, lane + LANES // 2, inner[part])
    for other in range(sums_ref.shape[0]):
        sums_ref[other] = sums


def norm_factors(sums):
    half = LANES // 2
    square, inner = sums[:, :half], sums[:, half:]
    rinv = lax.rsqrt(square / D + 1e-05)
    return rinv, rinv * rinv * rinv * inner / D


def spread(array, lane):
    return jnp.broadcast_to(array[:, lane : lane + 1], (ROWS, LANES))


def backward_kernel(
    table_ref,
    sums_ref,
    query_ref,
    cot_ref,
    mixer_ref,
    adjoint_ref,
    send_ref,
    totals_ref,
    scale_ref,
    shift_ref,
):
    tokens, width = query_ref.shape
    tiles, groups = tokens // TILE, width // LANES
    table = Table(table_ref, tiles, groups)
    sums = total(sums_ref[other] for other in range(sums_ref.shape[0]))
    totals_ref[...] = sums
    rinv, lean = norm_factors(sums)
    fulls = []
    for group in range(groups):
        lanes = lane_group(group)
        rate = table.rate(group)
        factors = per_mode(jnp.exp(-rate * ROWS))
        powers = phase_powers(rate, 0, 1)
        gain = jnp.broadcast_to(table.gain(group), (PAIR, LANES))
        states = (jnp.zeros((ROWS, LANES), F32),) * MODES
        for tile in reversed(range(tiles)):
            if tile < tiles - 1:
                alive = table.alive(tile + 1)
                states = tuple(s * alive for s in states)
            for step in reversed(range(0, TILE, PAIR)):
                rows = slice(tile * TILE + step, tile * TILE + step + PAIR)
                query = query_ref[rows, lanes].astype(F32)
                if group == 0:
                    for half in range(2):
                        lane, part = (tile * TILE + step) // ROWS + half, pl.ds(rows.start + half * ROWS, ROWS)
                        scale_ref[part, :] = spread(rinv, lane)
                        shift_ref[part, :] = spread(lean, lane)
                gated = query * mixer_ref[rows, lanes].astype(F32)
                scaled = cot_ref[rows, lanes].astype(F32) * gain
                adjoint = ((scale_ref[rows, :] * scaled - gated * shift_ref[rows, :]) * query).astype(BF16)
                adjoint_ref[rows, lanes] = adjoint
                x = adjoint.astype(F32)
                states = advance(factors, states, x[ROWS:])
                states = advance(factors, states, x[:ROWS])
        fulls.append(gather_phases(states, powers))
    send_state(fulls, send_ref)


def outputs_kernel(
    table_ref, totals_ref, query_ref, cot_ref, mixer_ref, mixed_ref, grad_query_ref, done_ref, scale_ref, shift_ref
):
    tokens, width = query_ref.shape
    tiles, groups = tokens // TILE, width // LANES
    table = Table(table_ref, tiles, groups)
    rinv, lean = norm_factors(totals_ref[...])
    for lane in range(tokens // ROWS):
        rows = slice(lane * ROWS, (lane + 1) * ROWS)
        scale_ref[rows, :] = spread(rinv, lane)
        shift_ref[rows, :] = spread(lean, lane)
    for group in range(groups):
        lanes = lane_group(group)
        gain = jnp.broadcast_to(table.gain(group), (TILE, LANES))
        for tile in range(tiles):
            rows = slice(tile * TILE, (tile + 1) * TILE)
            scale, shift = scale_ref[rows, :], shift_ref[rows, :]
            mixer = mixer_ref[rows, lanes].astype(F32)
            gated = query_ref[rows, lanes].astype(F32) * mixer
            scaled = cot_ref[rows, lanes].astype(F32) * gain
            mixed_ref[rows, lanes] = (gated * scale * gain).astype(BF16)
            grad_query_ref[rows, lanes] = ((scale * scaled - gated * shift) * mixer).astype(BF16)
    done_ref[...] = totals_ref[...]


def backward_local_kernel(
    starts_ref, table_ref, adjoint_ref, done_ref, head_ref, tail_ref, flags_ref, data_ref, work_ref
):
    tokens, width = adjoint_ref.shape
    tiles, groups = tokens // TILE, width // LANES
    me = lax.axis_index("seq")
    table = Table(table_ref, tiles, groups)
    for group in range(groups):
        put_tiles(data_ref, group, adjoint_ref[:, lane_group(group)].astype(F32))
        conv = head_ref.at[group] if group < HEAD else tail_ref.at[group - HEAD]
        rate, weight, skip = table.rate(group), table.weight(group), table.skip(group)
        local_conv(me, starts_ref, rate, weight, skip, data_ref, work_ref, conv, group, True)
    for part in range(starts_ref.shape[0] // tiles):
        put_flag(flags_ref, 2 * part, keeps(starts_ref, part * tiles, tiles))
        put_flag(flags_ref, 2 * part + 1, survive(starts_ref, part * tiles))


def backward_join_kernel(
    table_ref,
    flags_ref,
    got_ref,
    head_ref,
    tail_hbm,
    key_hbm,
    value_hbm,
    grad_key_hbm,
    grad_value_hbm,
    tail_ref,
    key_ref,
    value_ref,
    dproduct_ref,
    grad_key_ref,
    grad_value_ref,
    sems,
):
    tokens, width = key_hbm.shape
    tiles, groups = tokens // TILE, width // LANES
    table = Table(table_ref, tiles, groups)
    parts = got_ref.shape[0]
    me = lax.axis_index("seq")
    copies = Copies(sems)
    near = [copies.start(tail_hbm.at[group], tail_ref.at[group]) for group in range(groups - HEAD)]
    large = []
    for group in range(groups):
        lanes = lane_group(group)
        large.append(
            [
                copies.start(value_hbm.at[:, lanes], value_ref.at[group]),
                copies.start(key_hbm.at[:, lanes], key_ref.at[group]),
            ]
        )
    rates = [table.rate(group) for group in range(groups)]
    part_decay = [jnp.exp(-rate * tokens) for rate in rates]
    states = [jnp.zeros((MODES, LANES), F32)] * groups
    for part in range(parts - 1, 0, -1):
        kept, alive = get_flag(flags_ref, 2 * part), get_flag(flags_ref, 2 * part + 1)
        arrived = part_of(got_ref, part, groups)
        states = [
            jnp.where(part > me, a * alive + d * kept * s, s)
            for a, d, s in zip(arrived, part_decay, states)
        ]
    out = []

    def finish(group):
        lanes = lane_group(group)
        for copy in large[group]:
            copy.wait()
        grad_key_ref[group] = dproduct_ref[group] * value_ref[group]
        out.append(copies.start(grad_key_ref.at[group], grad_key_hbm.at[:, lanes]))
        grad_value_ref[group] = dproduct_ref[group] * key_ref[group]
        out.append(copies.start(grad_value_ref.at[group], grad_value_hbm.at[:, lanes]))

    for group in range(groups):
        lanes = lane_group(group)
        factors = per_mode(jnp.exp(-rates[group] * ROWS))
        carry = weighted(phase_powers(rates[group], ROWS, -1), states[group] * table.weight(group))
        if group >= HEAD:
            near[group - HEAD].wait()
        conv = head_ref.at[group] if group < HEAD else tail_ref.at[group - HEAD]
        for tile in reversed(range(tiles)):
            if tile < tiles - 1:
                alive = table.alive(tile + 1)
                carry = [c * alive for c in carry]
            for step in reversed(range(0, TILE, PAIR)):
                rows = slice(tile * TILE + step, tile * TILE + step + PAIR)
                extra = []
                for _ in range(2):
                    extra.append(total(carry))
                    carry = [c * f for c, f in zip(carry, factors)]
                dproduct = conv[rows, :] + jnp.concatenate(extra[::-1], axis=0)
                dproduct_ref[group, rows, :] = dproduct.astype(BF16)
        if group >= LAG:
            finish(group - LAG)
    for group in range(groups - LAG, groups):
        finish(group)
    for copy in out:
        copy.wait()


def scratch_of(item):
    if isinstance(item, tuple):
        return pltpu.VMEM(*item) if isinstance(item[0], tuple) else pltpu.VMEM(item, F32)
    return item


def call(kernel, ins, outs, scratch, work, vmem=16):
    return pl.pallas_call(
        kernel,
        out_shape=[jax.ShapeDtypeStruct(*out[:2]) for out in outs],
        in_specs=[pl.BlockSpec(memory_space=space) for _, space in ins],
        out_specs=[pl.BlockSpec(memory_space=(*out, pltpu.VMEM)[2]) for out in outs],
        scratch_shapes=[scratch_of(item) for item in scratch],
        compiler_params=pltpu.CompilerParams(vmem_limit_bytes=vmem * 1024 * 1024),
        cost_estimate=pl.CostEstimate(flops=work, bytes_accessed=work // 8, transcendentals=0),
    )(*[array for array, _ in ins])


def on_device(
    query_feat,
    key_feat,
    value_feat,
    decay_rate,
    residues,
    skip_gain,
    norm_gain,
    doc_starts,
    cotangent,
):
    tokens, width = query_feat.shape
    parts, peers = lax.axis_size("seq"), lax.axis_size("chan")
    tiles, groups = tokens // TILE, width // LANES
    starts = (doc_starts, pltpu.SMEM)
    weight = residues * jnp.sqrt(-jnp.expm1(-2.0 * decay_rate))
    skip, gain = skip_gain[None], norm_gain[None]
    whole, split, pitched = (tokens, width), (groups, tokens, LANES), (groups, tiles * PITCH, LANES)
    block, spread, summed = (parts, groups * MODES, LANES), (tokens, LANES), (peers, ROWS, LANES)
    modes, packed = (MODES, width), (table_rows(tiles, groups, parts), LANES)
    head_split, tail_split = (HEAD, tokens, LANES), (groups - HEAD, tokens, LANES)
    work = tokens * width

    def vmem(*arrays):
        return [(array, pltpu.VMEM) for array in arrays]

    def hbm(*arrays):
        return [(array, pl.ANY) for array in arrays]

    def sems(count):
        return pltpu.SemaphoreType.DMA((count,))

    (send,) = call(
        first_kernel,
        hbm(doc_starts, key_feat, value_feat, decay_rate),
        [(block, SEND)],
        [
            pltpu.SMEM(doc_starts.shape, jnp.int32),
            (split, BF16),
            (split, BF16),
            modes,
            sems(2 * groups + 2),
        ],
        work * 20,
        60,
    )
    got = lax.all_to_all(send, "seq", 0, 0)
    conv, table = call(
        forward_local_kernel,
        [starts] + vmem(key_feat, value_feat, decay_rate, weight, gain, skip),
        [(split, F32), (packed, F32)],
        [pitched, pitched],
        work * 50,
    )
    mixer, sums = call(
        forward_join_kernel,
        vmem(table, got, conv, query_feat, cotangent),
        [(whole, BF16), (summed, F32)],
        [spread, spread],
        work * 30,
    )
    sums = lax.all_to_all(sums, "chan", 0, 0)
    adjoint, send, totals = call(
        backward_kernel,
        vmem(table, sums, query_feat, cotangent, mixer),
        [(whole, BF16), (block, SEND), ((ROWS, LANES), F32)],
        [spread, spread],
        work * 30,
    )
    got = lax.all_to_all(send, "seq", 0, 0)
    mixed, grad_query, done = call(
        outputs_kernel,
        vmem(table, totals, query_feat, cotangent, mixer),
        [(whole, BF16), (whole, BF16), ((ROWS, LANES), F32)],
        [spread, spread],
        work * 20,
    )
    head, tail, flags = call(
        backward_local_kernel,
        [starts] + vmem(table, adjoint, done),
        [(head_split, F32), (tail_split, F32), ((2 * parts, LANES), F32)],
        [pitched, pitched],
        work * 50,
    )
    grad_key, grad_value = call(
        backward_join_kernel,
        vmem(table, flags, got, head) + hbm(tail, key_feat, value_feat),
        [(whole, BF16, pl.ANY), (whole, BF16, pl.ANY)],
        [tail_split] + [(split, BF16)] * 5 + [sems(5 * groups - HEAD)],
        work * 30,
        53,
    )
    return mixed, grad_query, grad_key, grad_value


def solution(mesh):
    both = P("seq", "chan")
    in_specs = (
        both,
        both,
        both,
        P(None, "chan"),
        P(None, "chan"),
        P("chan"),
        P("chan"),
        P(),
        both,
    )
    return jax.shard_map(
        on_device, mesh=mesh, in_specs=in_specs, out_specs=(both,) * 4, check_vma=False
    )
```

```python
import functools

import jax
import jax.numpy as jnp
from jax import lax
from jax.experimental import pallas as pl
from jax.experimental.pallas import tpu as pltpu
from jax.sharding import PartitionSpec as P


D = 8192
MODES = 8
TILE = 64
LANES = 128
ROWS = 8
PAIR = 2 * ROWS
PITCH = TILE + MODES

GROUP_ROWS = 24
GAIN, SKIP = 16, 17
F32 = jnp.float32
BF16 = jnp.bfloat16
SEND = BF16
UNROLL = 16
LAG = 3
HEAD = 2


def rounded(array):
    return array.astype(BF16).astype(F32)


def lane_group(group):
    return slice(group * LANES, (group + 1) * LANES)


def rows_of(tile):
    return slice(tile * MODES, (tile + 1) * MODES)


def survive(starts_ref, index):
    return (1 - starts_ref[index]).astype(F32)


def keeps(starts_ref, first, count):
    found = starts_ref[first]
    for step in range(1, count):
        found = found + starts_ref[first + step]
    return jnp.where(found == 0, 1.0, 0.0)


def total(parts):
    parts = list(parts)
    while len(parts) > 1:
        parts = [sum(parts[i : i + 2][1:], parts[i]) for i in range(0, len(parts), 2)]
    return parts[0]


def wide(table, m):
    return jnp.broadcast_to(table[m : m + 1], (ROWS, LANES))


def per_mode(table):
    return [wide(table, m) for m in range(MODES)]


def phase_powers(rate, first, sign):
    power = lax.broadcasted_iota(jnp.int32, (ROWS, LANES), 0).astype(F32) * sign + first
    return [jnp.exp(-wide(rate, m) * power) for m in range(MODES)]


def weighted(powers, table):
    return [p * wide(table, m) for m, p in enumerate(powers)]


def advance(factors, states, x):
    return tuple(f * s + x for f, s in zip(factors, states))


class Copies:
    def __init__(self, sems):
        self.sems, self.used = sems, 0

    def start(self, source, target):
        copy = pltpu.make_async_copy(source, target, self.sems.at[self.used])
        self.used += 1
        copy.start()
        return copy


def send_state(states, send_ref):
    block = jnp.concatenate(states, axis=0).astype(send_ref.dtype)
    for other in range(send_ref.shape[0]):
        send_ref[other] = block


def gather_phases(states, powers):
    return jnp.concatenate(
        [jnp.sum(s * p, axis=0, keepdims=True) for s, p in zip(states, powers)], axis=0
    )


def first_kernel(
    starts_hbm,
    key_hbm,
    value_hbm,
    rate_hbm,
    send_ref,
    starts_ref,
    key_ref,
    value_ref,
    rate_ref,
    sems,
):
    tokens, width = key_hbm.shape
    tiles, groups = tokens // TILE, width // LANES
    me = lax.axis_index("seq")
    copies = Copies(sems)
    large = []
    for group in range(groups):
        lanes = lane_group(group)
        large.append(
            [
                copies.start(key_hbm.at[:, lanes], key_ref.at[group]),
                copies.start(value_hbm.at[:, lanes], value_ref.at[group]),
            ]
        )
        if group == 0:
            small = [copies.start(rate_hbm, rate_ref), copies.start(starts_hbm, starts_ref)]
    for copy in small:
        copy.wait()
    fulls = []
    for group in range(groups):
        rate = rate_ref[:, lane_group(group)]
        factors = per_mode(jnp.exp(-rate * ROWS))
        powers = phase_powers(rate, ROWS - 1, -1)
        for copy in large[group]:
            copy.wait()
        states = (jnp.zeros((ROWS, LANES), F32),) * MODES
        for tile in range(tiles):
            if tile:
                alive = survive(starts_ref, me * tiles + tile)
                states = tuple(s * alive for s in states)
            for step in range(0, TILE, PAIR):
                rows = slice(tile * TILE + step, tile * TILE + step + PAIR)
                x = (key_ref[group, rows, :] * value_ref[group, rows, :]).astype(F32)
                states = advance(factors, states, x[:ROWS])
                states = advance(factors, states, x[ROWS:])
        fulls.append(gather_phases(states, powers))
    send_state(fulls, send_ref)


def per_tile(table, tiles):
    return [jnp.broadcast_to(table[m : m + 1], (tiles, LANES)) for m in range(MODES)]


def over_tile(step, first, reverse):
    def body(index, carry):
        return step(TILE - 1 - index if reverse else index, carry)

    return lax.fori_loop(0, TILE, body, first, unroll=UNROLL)


def tile_rows(tile, count=TILE, first=0):
    return slice(tile * PITCH + first, tile * PITCH + first + count)


def put_tiles(ref, group, data):
    for tile in range(data.shape[0] // TILE):
        ref[group, tile_rows(tile), :] = data[tile * TILE : (tile + 1) * TILE]


def local_conv(me, starts_ref, rate, weight, skip, data_ref, work_ref, conv_ref, group, reverse):
    tiles = data_ref.shape[1] // PITCH
    factors, weights = per_tile(jnp.exp(-rate), tiles), per_tile(weight, tiles)
    skip = jnp.broadcast_to(skip, (tiles, LANES))

    def rows(offset):
        return pl.ds(offset, tiles, stride=PITCH)

    def leave(offset, states):
        return advance(factors, states, data_ref[group, rows(offset), :])

    ends = over_tile(leave, (jnp.zeros((tiles, LANES), F32),) * MODES, reverse)
    for m in range(MODES):
        work_ref[group, rows(TILE + m), :] = ends[m]
    tile_decay = jnp.exp(-rate * TILE)
    state = jnp.zeros((MODES, LANES), F32)
    for tile in reversed(range(tiles)) if reverse else range(tiles):
        alive = survive(starts_ref, me * tiles + tile)
        here = tile_rows(tile, MODES, TILE)
        end = work_ref[group, here, :]
        if reverse:
            work_ref[group, here, :] = state
            state = (end + tile_decay * state) * alive
        else:
            state = state * alive
            work_ref[group, here, :] = state
            state = end + tile_decay * state

    def step(offset, states):
        x = data_ref[group, rows(offset), :]
        states = advance(factors, states, x)
        work_ref[group, rows(offset), :] = total(w * s for w, s in zip(weights, states)) + skip * x
        return states

    over_tile(step, tuple(work_ref[group, rows(TILE + m), :] for m in range(MODES)), reverse)
    for tile in range(tiles):
        conv_ref[tile * TILE : (tile + 1) * TILE, :] = work_ref[group, tile_rows(tile), :]


def table_rows(tiles, groups, parts):
    return groups * GROUP_ROWS + tiles + parts


def put_flag(ref, row, value):
    ref[row : row + 1, :] = jnp.full((1, LANES), value)


def get_flag(ref, row):
    return jnp.broadcast_to(ref[row : row + 1, :], (ROWS, LANES))


class Table:
    def __init__(self, ref, tiles, groups):
        self.ref, self.groups = ref, groups
        self.flags = groups * GROUP_ROWS
        self.parts = self.flags + tiles

    def rows(self, group, first, count):
        first += group * GROUP_ROWS
        return slice(first, first + count)

    def rate(self, group):
        return self.ref[self.rows(group, 0, MODES), :]

    def weight(self, group):
        return self.ref[self.rows(group, MODES, MODES), :]

    def gain(self, group):
        return self.ref[self.rows(group, GAIN, 1), :]

    def skip(self, group):
        return self.ref[self.rows(group, SKIP, 1), :]

    def alive(self, tile):
        return get_flag(self.ref, self.flags + tile)

    def kept(self, part):
        return get_flag(self.ref, self.parts + part)


def forward_local_kernel(
    starts_ref,
    key_ref,
    value_ref,
    rate_ref,
    weight_ref,
    gain_ref,
    skip_ref,
    conv_ref,
    table_ref,
    data_ref,
    work_ref,
):
    tokens, width = key_ref.shape
    tiles, groups = tokens // TILE, width // LANES
    me = lax.axis_index("seq")
    table = Table(table_ref, tiles, groups)
    for group in range(groups):
        lanes = lane_group(group)
        put_tiles(data_ref, group, rounded(key_ref[:, lanes].astype(F32) * value_ref[:, lanes].astype(F32)))
        rate, weight, skip = rate_ref[:, lanes], weight_ref[:, lanes], skip_ref[:, lanes]
        local_conv(me, starts_ref, rate, weight, skip, data_ref, work_ref, conv_ref.at[group], group, False)
        table_ref[table.rows(group, 0, MODES), :] = rate
        table_ref[table.rows(group, MODES, MODES), :] = weight
        table_ref[table.rows(group, GAIN, 1), :] = gain_ref[:, lanes]
        table_ref[table.rows(group, SKIP, 1), :] = skip
    for tile in range(tiles):
        put_flag(table_ref, table.flags + tile, survive(starts_ref, me * tiles + tile))
    for part in range(starts_ref.shape[0] // tiles):
        put_flag(table_ref, table.parts + part, keeps(starts_ref, part * tiles, tiles))


def put_sums(sums, lane, array):
    lanes = lax.broadcasted_iota(jnp.int32, (ROWS, LANES), 1)
    return jnp.where(lanes == lane, jnp.sum(array, axis=1, keepdims=True), sums)


def part_of(got_ref, part, groups):
    return [got_ref[part, rows_of(group), :].astype(F32) for group in range(groups)]


def forward_join_kernel(
    table_ref,
    got_ref,
    conv_ref,
    query_ref,
    cot_ref,
    mixer_ref,
    sums_ref,
    square_ref,
    inner_ref,
):
    tokens, width = query_ref.shape
    tiles, groups = tokens // TILE, width // LANES
    table = Table(table_ref, tiles, groups)
    parts = got_ref.shape[0]
    me = lax.axis_index("seq")
    rates = [table.rate(group) for group in range(groups)]
    sums = jnp.zeros((ROWS, LANES), F32)
    part_decay = [jnp.exp(-rate * tokens) for rate in rates]
    states = [jnp.zeros((MODES, LANES), F32)] * groups
    for part in range(parts - 1):
        kept = table.kept(part)
        arrived = part_of(got_ref, part, groups)
        states = [
            jnp.where(part < me, a + d * kept * s, s) for a, d, s in zip(arrived, part_decay, states)
        ]
    for group in range(groups):
        lanes = lane_group(group)
        factors = per_mode(jnp.exp(-rates[group] * ROWS))
        carry = weighted(phase_powers(rates[group], 1, 1), states[group] * table.weight(group))
        gain = jnp.broadcast_to(table.gain(group), (PAIR, LANES))
        for tile in range(tiles):
            alive = table.alive(tile)
            carry = [c * alive for c in carry]
            for step in range(0, TILE, PAIR):
                rows = slice(tile * TILE + step, tile * TILE + step + PAIR)
                extra = []
                for _ in range(2):
                    extra.append(total(carry))
                    carry = [c * f for c, f in zip(carry, factors)]
                mixer = (conv_ref[group, rows, :] + jnp.concatenate(extra, axis=0)).astype(BF16)
                mixer_ref[rows, lanes] = mixer
                gated = query_ref[rows, lanes].astype(F32) * mixer.astype(F32)
                square = gated * gated
                inner = cot_ref[rows, lanes].astype(F32) * gain * gated
                if group:
                    square, inner = square + square_ref[rows, :], inner + inner_ref[rows, :]
                if group < groups - 1:
                    square_ref[rows, :] = square
                    inner_ref[rows, :] = inner
                    continue
                for half in range(2):
                    lane, part = (tile * TILE + step) // ROWS + half, slice(half * ROWS, (half + 1) * ROWS)
                    sums = put_sums(sums, lane, square[part])
                    sums = put_sums(sums, lane + LANES // 2, inner[part])
    for other in range(sums_ref.shape[0]):
        sums_ref[other] = sums


def norm_factors(sums):
    half = LANES // 2
    square, inner = sums[:, :half], sums[:, half:]
    rinv = lax.rsqrt(square / D + 1e-05)
    return rinv, rinv * rinv * rinv * inner / D


def spread(array, lane):
    return jnp.broadcast_to(array[:, lane : lane + 1], (ROWS, LANES))


def backward_kernel(
    table_ref,
    sums_ref,
    query_ref,
    cot_ref,
    mixer_ref,
    adjoint_ref,
    send_ref,
    totals_ref,
    scale_ref,
    shift_ref,
):
    tokens, width = query_ref.shape
    tiles, groups = tokens // TILE, width // LANES
    table = Table(table_ref, tiles, groups)
    sums = total(sums_ref[other] for other in range(sums_ref.shape[0]))
    totals_ref[...] = sums
    rinv, lean = norm_factors(sums)
    fulls = []
    for group in range(groups):
        lanes = lane_group(group)
        rate = table.rate(group)
        factors = per_mode(jnp.exp(-rate * ROWS))
        powers = phase_powers(rate, 0, 1)
        gain = jnp.broadcast_to(table.gain(group), (PAIR, LANES))
        states = (jnp.zeros((ROWS, LANES), F32),) * MODES
        for tile in reversed(range(tiles)):
            if tile < tiles - 1:
                alive = table.alive(tile + 1)
                states = tuple(s * alive for s in states)
            for step in reversed(range(0, TILE, PAIR)):
                rows = slice(tile * TILE + step, tile * TILE + step + PAIR)
                query = query_ref[rows, lanes].astype(F32)
                if group == 0:
                    for half in range(2):
                        lane, part = (tile * TILE + step) // ROWS + half, pl.ds(rows.start + half * ROWS, ROWS)
                        scale_ref[part, :] = spread(rinv, lane)
                        shift_ref[part, :] = spread(lean, lane)
                gated = query * mixer_ref[rows, lanes].astype(F32)
                scaled = cot_ref[rows, lanes].astype(F32) * gain
                adjoint = ((scale_ref[rows, :] * scaled - gated * shift_ref[rows, :]) * query).astype(BF16)
                adjoint_ref[rows, lanes] = adjoint
                x = adjoint.astype(F32)
                states = advance(factors, states, x[ROWS:])
                states = advance(factors, states, x[:ROWS])
        fulls.append(gather_phases(states, powers))
    send_state(fulls, send_ref)


def outputs_kernel(
    table_ref, totals_ref, query_ref, cot_ref, mixer_ref, mixed_ref, grad_query_ref, done_ref, scale_ref, shift_ref
):
    tokens, width = query_ref.shape
    tiles, groups = tokens // TILE, width // LANES
    table = Table(table_ref, tiles, groups)
    rinv, lean = norm_factors(totals_ref[...])
    for lane in range(tokens // ROWS):
        rows = slice(lane * ROWS, (lane + 1) * ROWS)
        scale_ref[rows, :] = spread(rinv, lane)
        shift_ref[rows, :] = spread(lean, lane)
    for group in range(groups):
        lanes = lane_group(group)
        gain = jnp.broadcast_to(table.gain(group), (TILE, LANES))
        for tile in range(tiles):
            rows = slice(tile * TILE, (tile + 1) * TILE)
            scale, shift = scale_ref[rows, :], shift_ref[rows, :]
            mixer = mixer_ref[rows, lanes].astype(F32)
            gated = query_ref[rows, lanes].astype(F32) * mixer
            scaled = cot_ref[rows, lanes].astype(F32) * gain
            mixed_ref[rows, lanes] = (gated * scale * gain).astype(BF16)
            grad_query_ref[rows, lanes] = ((scale * scaled - gated * shift) * mixer).astype(BF16)
    done_ref[...] = totals_ref[...]


def backward_local_kernel(
    starts_ref, table_ref, adjoint_ref, done_ref, head_ref, tail_ref, flags_ref, data_ref, work_ref
):
    tokens, width = adjoint_ref.shape
    tiles, groups = tokens // TILE, width // LANES
    me = lax.axis_index("seq")
    table = Table(table_ref, tiles, groups)
    for group in range(groups):
        put_tiles(data_ref, group, adjoint_ref[:, lane_group(group)].astype(F32))
        conv = head_ref.at[group] if group < HEAD else tail_ref.at[group - HEAD]
        rate, weight, skip = table.rate(group), table.weight(group), table.skip(group)
        local_conv(me, starts_ref, rate, weight, skip, data_ref, work_ref, conv, group, True)
    for part in range(starts_ref.shape[0] // tiles):
        put_flag(flags_ref, 2 * part, keeps(starts_ref, part * tiles, tiles))
        put_flag(flags_ref, 2 * part + 1, survive(starts_ref, part * tiles))


def backward_join_kernel(
    table_ref,
    flags_ref,
    got_ref,
    head_ref,
    tail_ref,
    key_hbm,
    value_hbm,
    grad_key_hbm,
    grad_value_hbm,
    key_ref,
    value_ref,
    dproduct_ref,
    grad_key_ref,
    grad_value_ref,
    sems,
):
    tokens, width = key_hbm.shape
    tiles, groups = tokens // TILE, width // LANES
    table = Table(table_ref, tiles, groups)
    parts = got_ref.shape[0]
    me = lax.axis_index("seq")
    copies = Copies(sems)
    large = []
    for group in range(groups):
        lanes = lane_group(group)
        large.append(
            [
                copies.start(value_hbm.at[:, lanes], value_ref.at[group]),
                copies.start(key_hbm.at[:, lanes], key_ref.at[group]),
            ]
        )
    rates = [table.rate(group) for group in range(groups)]
    part_decay = [jnp.exp(-rate * tokens) for rate in rates]
    states = [jnp.zeros((MODES, LANES), F32)] * groups
    for part in range(parts - 1, 0, -1):
        kept, alive = get_flag(flags_ref, 2 * part), get_flag(flags_ref, 2 * part + 1)
        arrived = part_of(got_ref, part, groups)
        states = [
            jnp.where(part > me, a * alive + d * kept * s, s)
            for a, d, s in zip(arrived, part_decay, states)
        ]
    out = []

    def finish(group):
        lanes = lane_group(group)
        for copy in large[group]:
            copy.wait()
        grad_key_ref[group] = dproduct_ref[group] * value_ref[group]
        out.append(copies.start(grad_key_ref.at[group], grad_key_hbm.at[:, lanes]))
        grad_value_ref[group] = dproduct_ref[group] * key_ref[group]
        out.append(copies.start(grad_value_ref.at[group], grad_value_hbm.at[:, lanes]))

    for group in range(groups):
        lanes = lane_group(group)
        factors = per_mode(jnp.exp(-rates[group] * ROWS))
        carry = weighted(phase_powers(rates[group], ROWS, -1), states[group] * table.weight(group))
        conv = head_ref.at[group] if group < HEAD else tail_ref.at[group - HEAD]
        for tile in reversed(range(tiles)):
            if tile < tiles - 1:
                alive = table.alive(tile + 1)
                carry = [c * alive for c in carry]
            for step in reversed(range(0, TILE, PAIR)):
                rows = slice(tile * TILE + step, tile * TILE + step + PAIR)
                extra = []
                for _ in range(2):
                    extra.append(total(carry))
                    carry = [c * f for c, f in zip(carry, factors)]
                dproduct = conv[rows, :] + jnp.concatenate(extra[::-1], axis=0)
                dproduct_ref[group, rows, :] = dproduct.astype(BF16)
        if group >= LAG:
            finish(group - LAG)
    for group in range(groups - LAG, groups):
        finish(group)
    for copy in out:
        copy.wait()


def scratch_of(item):
    if isinstance(item, tuple):
        return pltpu.VMEM(*item) if isinstance(item[0], tuple) else pltpu.VMEM(item, F32)
    return item


def call(kernel, ins, outs, scratch, work, vmem=16):
    return pl.pallas_call(
        kernel,
        out_shape=[jax.ShapeDtypeStruct(*out[:2]) for out in outs],
        in_specs=[pl.BlockSpec(memory_space=space) for _, space in ins],
        out_specs=[pl.BlockSpec(memory_space=(*out, pltpu.VMEM)[2]) for out in outs],
        scratch_shapes=[scratch_of(item) for item in scratch],
        compiler_params=pltpu.CompilerParams(vmem_limit_bytes=vmem * 1024 * 1024),
        cost_estimate=pl.CostEstimate(flops=work, bytes_accessed=work // 8, transcendentals=0),
    )(*[array for array, _ in ins])


def on_device(
    query_feat,
    key_feat,
    value_feat,
    decay_rate,
    residues,
    skip_gain,
    norm_gain,
    doc_starts,
    cotangent,
):
    tokens, width = query_feat.shape
    parts, peers = lax.axis_size("seq"), lax.axis_size("chan")
    tiles, groups = tokens // TILE, width // LANES
    starts = (doc_starts, pltpu.SMEM)
    weight = residues * jnp.sqrt(-jnp.expm1(-2.0 * decay_rate))
    skip, gain = skip_gain[None], norm_gain[None]
    whole, split, pitched = (tokens, width), (groups, tokens, LANES), (groups, tiles * PITCH, LANES)
    block, spread, summed = (parts, groups * MODES, LANES), (tokens, LANES), (peers, ROWS, LANES)
    modes, packed = (MODES, width), (table_rows(tiles, groups, parts), LANES)
    head_split, tail_split = (HEAD, tokens, LANES), (groups - HEAD, tokens, LANES)
    work = tokens * width

    def vmem(*arrays):
        return [(array, pltpu.VMEM) for array in arrays]

    def hbm(*arrays):
        return [(array, pl.ANY) for array in arrays]

    def sems(count):
        return pltpu.SemaphoreType.DMA((count,))

    (send,) = call(
        first_kernel,
        hbm(doc_starts, key_feat, value_feat, decay_rate),
        [(block, SEND)],
        [
            pltpu.SMEM(doc_starts.shape, jnp.int32),
            (split, BF16),
            (split, BF16),
            modes,
            sems(2 * groups + 2),
        ],
        work * 20,
        60,
    )
    got = lax.all_to_all(send, "seq", 0, 0)
    conv, table = call(
        forward_local_kernel,
        [starts] + vmem(key_feat, value_feat, decay_rate, weight, gain, skip),
        [(split, F32), (packed, F32)],
        [pitched, pitched],
        work * 50,
    )
    mixer, sums = call(
        forward_join_kernel,
        vmem(table, got, conv, query_feat, cotangent),
        [(whole, BF16), (summed, F32)],
        [spread, spread],
        work * 30,
    )
    sums = lax.all_to_all(sums, "chan", 0, 0)
    adjoint, send, totals = call(
        backward_kernel,
        vmem(table, sums, query_feat, cotangent, mixer),
        [(whole, BF16), (block, SEND), ((ROWS, LANES), F32)],
        [spread, spread],
        work * 30,
    )
    got = lax.all_to_all(send, "seq", 0, 0)
    mixed, grad_query, done = call(
        outputs_kernel,
        vmem(table, totals, query_feat, cotangent, mixer),
        [(whole, BF16), (whole, BF16), ((ROWS, LANES), F32)],
        [spread, spread],
        work * 20,
    )
    head, tail, flags = call(
        backward_local_kernel,
        [starts] + vmem(table, adjoint, done),
        [(head_split, F32), (tail_split, F32), ((2 * parts, LANES), F32)],
        [pitched, pitched],
        work * 50,
    )
    grad_key, grad_value = call(
        backward_join_kernel,
        vmem(table, flags, got, head, tail) + hbm(key_feat, value_feat),
        [(whole, BF16, pl.ANY), (whole, BF16, pl.ANY)],
        [(split, BF16)] * 5 + [sems(4 * groups)],
        work * 30,
        52,
    )
    return mixed, grad_query, grad_key, grad_value


def solution(mesh):
    both = P("seq", "chan")
    in_specs = (
        both,
        both,
        both,
        P(None, "chan"),
        P(None, "chan"),
        P("chan"),
        P("chan"),
        P(),
        both,
    )
    return jax.shard_map(
        on_device, mesh=mesh, in_specs=in_specs, out_specs=(both,) * 4, check_vma=False
    )
```

```python
import functools

import jax
import jax.numpy as jnp
from jax import lax
from jax.experimental import pallas as pl
from jax.experimental.pallas import tpu as pltpu
from jax.sharding import PartitionSpec as P


D = 8192
MODES = 8
TILE = 64
LANES = 128
ROWS = 8
PAIR = 2 * ROWS
PITCH = TILE + MODES

GROUP_ROWS = 24
GAIN, SKIP = 16, 17
F32 = jnp.float32
BF16 = jnp.bfloat16
SEND = BF16
UNROLL = 16
LAG = 3
HEAD = 2


def rounded(array):
    return array.astype(BF16).astype(F32)


def lane_group(group):
    return slice(group * LANES, (group + 1) * LANES)


def rows_of(tile):
    return slice(tile * MODES, (tile + 1) * MODES)


def survive(starts_ref, index):
    return (1 - starts_ref[index]).astype(F32)


def keeps(starts_ref, first, count):
    found = starts_ref[first]
    for step in range(1, count):
        found = found + starts_ref[first + step]
    return jnp.where(found == 0, 1.0, 0.0)


def total(parts):
    parts = list(parts)
    while len(parts) > 1:
        parts = [sum(parts[i : i + 2][1:], parts[i]) for i in range(0, len(parts), 2)]
    return parts[0]


def wide(table, m):
    return jnp.broadcast_to(table[m : m + 1], (ROWS, LANES))


def per_mode(table):
    return [wide(table, m) for m in range(MODES)]


def phase_powers(rate, first, sign):
    power = lax.broadcasted_iota(jnp.int32, (ROWS, LANES), 0).astype(F32) * sign + first
    return [jnp.exp(-wide(rate, m) * power) for m in range(MODES)]


def weighted(powers, table):
    return [p * wide(table, m) for m, p in enumerate(powers)]


def advance(factors, states, x):
    return tuple(f * s + x for f, s in zip(factors, states))


class Copies:
    def __init__(self, sems):
        self.sems, self.used = sems, 0

    def start(self, source, target):
        copy = pltpu.make_async_copy(source, target, self.sems.at[self.used])
        self.used += 1
        copy.start()
        return copy


def send_state(states, send_ref):
    block = jnp.concatenate(states, axis=0).astype(send_ref.dtype)
    for other in range(send_ref.shape[0]):
        send_ref[other] = block


def gather_phases(states, powers):
    return jnp.concatenate(
        [jnp.sum(s * p, axis=0, keepdims=True) for s, p in zip(states, powers)], axis=0
    )


def first_kernel(
    starts_hbm,
    key_hbm,
    value_hbm,
    rate_hbm,
    send_ref,
    starts_ref,
    key_ref,
    value_ref,
    rate_ref,
    sems,
):
    tokens, width = key_hbm.shape
    tiles, groups = tokens // TILE, width // LANES
    me = lax.axis_index("seq")
    copies = Copies(sems)
    large = []
    for group in range(groups):
        lanes = lane_group(group)
        large.append(
            [
                copies.start(key_hbm.at[:, lanes], key_ref.at[group]),
                copies.start(value_hbm.at[:, lanes], value_ref.at[group]),
            ]
        )
        if group == 0:
            small = [copies.start(rate_hbm, rate_ref), copies.start(starts_hbm, starts_ref)]
    for copy in small:
        copy.wait()
    fulls = []
    for group in range(groups):
        rate = rate_ref[:, lane_group(group)]
        factors = per_mode(jnp.exp(-rate * ROWS))
        powers = phase_powers(rate, ROWS - 1, -1)
        for copy in large[group]:
            copy.wait()
        states = (jnp.zeros((ROWS, LANES), F32),) * MODES
        for tile in range(tiles):
            if tile:
                alive = survive(starts_ref, me * tiles + tile)
                states = tuple(s * alive for s in states)
            for step in range(0, TILE, PAIR):
                rows = slice(tile * TILE + step, tile * TILE + step + PAIR)
                x = (key_ref[group, rows, :] * value_ref[group, rows, :]).astype(F32)
                states = advance(factors, states, x[:ROWS])
                states = advance(factors, states, x[ROWS:])
        fulls.append(gather_phases(states, powers))
    send_state(fulls, send_ref)


def per_tile(table, tiles):
    return [jnp.broadcast_to(table[m : m + 1], (tiles, LANES)) for m in range(MODES)]


def over_tile(step, first, reverse):
    def body(index, carry):
        return step(TILE - 1 - index if reverse else index, carry)

    return lax.fori_loop(0, TILE, body, first, unroll=UNROLL)


def tile_rows(tile, count=TILE, first=0):
    return slice(tile * PITCH + first, tile * PITCH + first + count)


def put_tiles(ref, group, data):
    for tile in range(data.shape[0] // TILE):
        ref[group, tile_rows(tile), :] = data[tile * TILE : (tile + 1) * TILE]


def local_conv(me, starts_ref, rate, weight, skip, data_ref, work_ref, conv_ref, group, reverse):
    tiles = data_ref.shape[1] // PITCH
    factors, weights = per_tile(jnp.exp(-rate), tiles), per_tile(weight, tiles)
    skip = jnp.broadcast_to(skip, (tiles, LANES))

    def rows(offset):
        return pl.ds(offset, tiles, stride=PITCH)

    def leave(offset, states):
        return advance(factors, states, data_ref[group, rows(offset), :])

    ends = over_tile(leave, (jnp.zeros((tiles, LANES), F32),) * MODES, reverse)
    for m in range(MODES):
        work_ref[group, rows(TILE + m), :] = ends[m]
    tile_decay = jnp.exp(-rate * TILE)
    state = jnp.zeros((MODES, LANES), F32)
    for tile in reversed(range(tiles)) if reverse else range(tiles):
        alive = survive(starts_ref, me * tiles + tile)
        here = tile_rows(tile, MODES, TILE)
        end = work_ref[group, here, :]
        if reverse:
            work_ref[group, here, :] = state
            state = (end + tile_decay * state) * alive
        else:
            state = state * alive
            work_ref[group, here, :] = state
            state = end + tile_decay * state

    def step(offset, states):
        x = data_ref[group, rows(offset), :]
        states = advance(factors, states, x)
        work_ref[group, rows(offset), :] = total(w * s for w, s in zip(weights, states)) + skip * x
        return states

    over_tile(step, tuple(work_ref[group, rows(TILE + m), :] for m in range(MODES)), reverse)
    for tile in range(tiles):
        conv_ref[tile * TILE : (tile + 1) * TILE, :] = work_ref[group, tile_rows(tile), :]


def table_rows(tiles, groups, parts):
    return groups * GROUP_ROWS + tiles + parts


def put_flag(ref, row, value):
    ref[row : row + 1, :] = jnp.full((1, LANES), value)


def get_flag(ref, row):
    return jnp.broadcast_to(ref[row : row + 1, :], (ROWS, LANES))


class Table:
    def __init__(self, ref, tiles, groups):
        self.ref, self.groups = ref, groups
        self.flags = groups * GROUP_ROWS
        self.parts = self.flags + tiles

    def rows(self, group, first, count):
        first += group * GROUP_ROWS
        return slice(first, first + count)

    def rate(self, group):
        return self.ref[self.rows(group, 0, MODES), :]

    def weight(self, group):
        return self.ref[self.rows(group, MODES, MODES), :]

    def gain(self, group):
        return self.ref[self.rows(group, GAIN, 1), :]

    def skip(self, group):
        return self.ref[self.rows(group, SKIP, 1), :]

    def alive(self, tile):
        return get_flag(self.ref, self.flags + tile)

    def kept(self, part):
        return get_flag(self.ref, self.parts + part)


def forward_local_kernel(
    starts_ref,
    key_ref,
    value_ref,
    rate_ref,
    weight_ref,
    gain_ref,
    skip_ref,
    conv_ref,
    table_ref,
    data_ref,
    work_ref,
):
    tokens, width = key_ref.shape
    tiles, groups = tokens // TILE, width // LANES
    me = lax.axis_index("seq")
    table = Table(table_ref, tiles, groups)
    for group in range(groups):
        lanes = lane_group(group)
        put_tiles(data_ref, group, rounded(key_ref[:, lanes].astype(F32) * value_ref[:, lanes].astype(F32)))
        rate, weight, skip = rate_ref[:, lanes], weight_ref[:, lanes], skip_ref[:, lanes]
        local_conv(me, starts_ref, rate, weight, skip, data_ref, work_ref, conv_ref.at[group], group, False)
        table_ref[table.rows(group, 0, MODES), :] = rate
        table_ref[table.rows(group, MODES, MODES), :] = weight
        table_ref[table.rows(group, GAIN, 1), :] = gain_ref[:, lanes]
        table_ref[table.rows(group, SKIP, 1), :] = skip
    for tile in range(tiles):
        put_flag(table_ref, table.flags + tile, survive(starts_ref, me * tiles + tile))
    for part in range(starts_ref.shape[0] // tiles):
        put_flag(table_ref, table.parts + part, keeps(starts_ref, part * tiles, tiles))


def put_sums(sums, lane, array):
    lanes = lax.broadcasted_iota(jnp.int32, (ROWS, LANES), 1)
    return jnp.where(lanes == lane, jnp.sum(array, axis=1, keepdims=True), sums)


def part_of(got_ref, part, groups):
    block = got_ref[part].astype(F32)
    return [block[rows_of(group)] for group in range(groups)]


def forward_join_kernel(
    table_ref,
    got_ref,
    conv_ref,
    query_ref,
    cot_ref,
    mixer_ref,
    sums_ref,
    square_ref,
    inner_ref,
):
    tokens, width = query_ref.shape
    tiles, groups = tokens // TILE, width // LANES
    table = Table(table_ref, tiles, groups)
    parts = got_ref.shape[0]
    me = lax.axis_index("seq")
    rates = [table.rate(group) for group in range(groups)]
    sums = jnp.zeros((ROWS, LANES), F32)
    part_decay = [jnp.exp(-rate * tokens) for rate in rates]
    states = [jnp.zeros((MODES, LANES), F32)] * groups
    for part in range(parts - 1):
        kept = table.kept(part)
        arrived = part_of(got_ref, part, groups)
        states = [
            jnp.where(part < me, a + d * kept * s, s) for a, d, s in zip(arrived, part_decay, states)
        ]
    for group in range(groups):
        lanes = lane_group(group)
        factors = per_mode(jnp.exp(-rates[group] * ROWS))
        carry = weighted(phase_powers(rates[group], 1, 1), states[group] * table.weight(group))
        gain = jnp.broadcast_to(table.gain(group), (PAIR, LANES))
        for tile in range(tiles):
            alive = table.alive(tile)
            carry = [c * alive for c in carry]
            for step in range(0, TILE, PAIR):
                rows = slice(tile * TILE + step, tile * TILE + step + PAIR)
                extra = []
                for _ in range(2):
                    extra.append(total(carry))
                    carry = [c * f for c, f in zip(carry, factors)]
                mixer = (conv_ref[group, rows, :] + jnp.concatenate(extra, axis=0)).astype(BF16)
                mixer_ref[rows, lanes] = mixer
                gated = query_ref[rows, lanes].astype(F32) * mixer.astype(F32)
                square = gated * gated
                inner = cot_ref[rows, lanes].astype(F32) * gain * gated
                if group:
                    square, inner = square + square_ref[rows, :], inner + inner_ref[rows, :]
                if group < groups - 1:
                    square_ref[rows, :] = square
                    inner_ref[rows, :] = inner
                    continue
                for half in range(2):
                    lane, part = (tile * TILE + step) // ROWS + half, slice(half * ROWS, (half + 1) * ROWS)
                    sums = put_sums(sums, lane, square[part])
                    sums = put_sums(sums, lane + LANES // 2, inner[part])
    for other in range(sums_ref.shape[0]):
        sums_ref[other] = sums


def norm_factors(sums):
    half = LANES // 2
    square, inner = sums[:, :half], sums[:, half:]
    rinv = lax.rsqrt(square / D + 1e-05)
    return rinv, rinv * rinv * rinv * inner / D


def spread(array, lane):
    return jnp.broadcast_to(array[:, lane : lane + 1], (ROWS, LANES))


def backward_kernel(
    table_ref,
    sums_ref,
    query_ref,
    cot_ref,
    mixer_ref,
    adjoint_ref,
    send_ref,
    totals_ref,
    scale_ref,
    shift_ref,
):
    tokens, width = query_ref.shape
    tiles, groups = tokens // TILE, width // LANES
    table = Table(table_ref, tiles, groups)
    sums = total(sums_ref[other] for other in range(sums_ref.shape[0]))
    totals_ref[...] = sums
    rinv, lean = norm_factors(sums)
    fulls = []
    for group in range(groups):
        lanes = lane_group(group)
        rate = table.rate(group)
        factors = per_mode(jnp.exp(-rate * ROWS))
        powers = phase_powers(rate, 0, 1)
        gain = jnp.broadcast_to(table.gain(group), (PAIR, LANES))
        states = (jnp.zeros((ROWS, LANES), F32),) * MODES
        for tile in reversed(range(tiles)):
            if tile < tiles - 1:
                alive = table.alive(tile + 1)
                states = tuple(s * alive for s in states)
            for step in reversed(range(0, TILE, PAIR)):
                rows = slice(tile * TILE + step, tile * TILE + step + PAIR)
                query = query_ref[rows, lanes].astype(F32)
                if group == 0:
                    for half in range(2):
                        lane, part = (tile * TILE + step) // ROWS + half, pl.ds(rows.start + half * ROWS, ROWS)
                        scale_ref[part, :] = spread(rinv, lane)
                        shift_ref[part, :] = spread(lean, lane)
                gated = query * mixer_ref[rows, lanes].astype(F32)
                scaled = cot_ref[rows, lanes].astype(F32) * gain
                adjoint = ((scale_ref[rows, :] * scaled - gated * shift_ref[rows, :]) * query).astype(BF16)
                adjoint_ref[rows, lanes] = adjoint
                x = adjoint.astype(F32)
                states = advance(factors, states, x[ROWS:])
                states = advance(factors, states, x[:ROWS])
        fulls.append(gather_phases(states, powers))
    send_state(fulls, send_ref)


def outputs_kernel(
    table_ref, totals_ref, query_ref, cot_ref, mixer_ref, mixed_ref, grad_query_ref, done_ref, scale_ref, shift_ref
):
    tokens, width = query_ref.shape
    tiles, groups = tokens // TILE, width // LANES
    table = Table(table_ref, tiles, groups)
    rinv, lean = norm_factors(totals_ref[...])
    for lane in range(tokens // ROWS):
        rows = slice(lane * ROWS, (lane + 1) * ROWS)
        scale_ref[rows, :] = spread(rinv, lane)
        shift_ref[rows, :] = spread(lean, lane)
    for group in range(groups):
        lanes = lane_group(group)
        gain = jnp.broadcast_to(table.gain(group), (TILE, LANES))
        for tile in range(tiles):
            rows = slice(tile * TILE, (tile + 1) * TILE)
            scale, shift = scale_ref[rows, :], shift_ref[rows, :]
            mixer = mixer_ref[rows, lanes].astype(F32)
            gated = query_ref[rows, lanes].astype(F32) * mixer
            scaled = cot_ref[rows, lanes].astype(F32) * gain
            mixed_ref[rows, lanes] = (gated * scale * gain).astype(BF16)
            grad_query_ref[rows, lanes] = ((scale * scaled - gated * shift) * mixer).astype(BF16)
    done_ref[...] = totals_ref[...]


def backward_local_kernel(
    starts_ref, table_ref, adjoint_ref, done_ref, head_ref, tail_ref, flags_ref, data_ref, work_ref
):
    tokens, width = adjoint_ref.shape
    tiles, groups = tokens // TILE, width // LANES
    me = lax.axis_index("seq")
    table = Table(table_ref, tiles, groups)
    for group in range(groups):
        put_tiles(data_ref, group, adjoint_ref[:, lane_group(group)].astype(F32))
        conv = head_ref.at[group] if group < HEAD else tail_ref.at[group - HEAD]
        rate, weight, skip = table.rate(group), table.weight(group), table.skip(group)
        local_conv(me, starts_ref, rate, weight, skip, data_ref, work_ref, conv, group, True)
    for part in range(starts_ref.shape[0] // tiles):
        put_flag(flags_ref, 2 * part, keeps(starts_ref, part * tiles, tiles))
        put_flag(flags_ref, 2 * part + 1, survive(starts_ref, part * tiles))


def backward_join_kernel(
    table_ref,
    flags_ref,
    got_ref,
    head_ref,
    tail_ref,
    key_hbm,
    value_hbm,
    grad_key_hbm,
    grad_value_hbm,
    key_ref,
    value_ref,
    dproduct_ref,
    grad_key_ref,
    grad_value_ref,
    sems,
):
    tokens, width = key_hbm.shape
    tiles, groups = tokens // TILE, width // LANES
    table = Table(table_ref, tiles, groups)
    parts = got_ref.shape[0]
    me = lax.axis_index("seq")
    copies = Copies(sems)
    large = []
    for group in range(groups):
        lanes = lane_group(group)
        large.append(
            [
                copies.start(value_hbm.at[:, lanes], value_ref.at[group]),
                copies.start(key_hbm.at[:, lanes], key_ref.at[group]),
            ]
        )
    rates = [table.rate(group) for group in range(groups)]
    part_decay = [jnp.exp(-rate * tokens) for rate in rates]
    states = [jnp.zeros((MODES, LANES), F32)] * groups
    for part in range(parts - 1, 0, -1):
        kept, alive = get_flag(flags_ref, 2 * part), get_flag(flags_ref, 2 * part + 1)
        arrived = part_of(got_ref, part, groups)
        states = [
            jnp.where(part > me, a * alive + d * kept * s, s)
            for a, d, s in zip(arrived, part_decay, states)
        ]
    out = []

    def finish(group):
        lanes = lane_group(group)
        for copy in large[group]:
            copy.wait()
        grad_key_ref[group] = dproduct_ref[group] * value_ref[group]
        out.append(copies.start(grad_key_ref.at[group], grad_key_hbm.at[:, lanes]))
        grad_value_ref[group] = dproduct_ref[group] * key_ref[group]
        out.append(copies.start(grad_value_ref.at[group], grad_value_hbm.at[:, lanes]))

    for group in range(groups):
        lanes = lane_group(group)
        factors = per_mode(jnp.exp(-rates[group] * ROWS))
        carry = weighted(phase_powers(rates[group], ROWS, -1), states[group] * table.weight(group))
        conv = head_ref.at[group] if group < HEAD else tail_ref.at[group - HEAD]
        for tile in reversed(range(tiles)):
            if tile < tiles - 1:
                alive = table.alive(tile + 1)
                carry = [c * alive for c in carry]
            for step in reversed(range(0, TILE, PAIR)):
                rows = slice(tile * TILE + step, tile * TILE + step + PAIR)
                extra = []
                for _ in range(2):
                    extra.append(total(carry))
                    carry = [c * f for c, f in zip(carry, factors)]
                dproduct = conv[rows, :] + jnp.concatenate(extra[::-1], axis=0)
                dproduct_ref[group, rows, :] = dproduct.astype(BF16)
        if group >= LAG:
            finish(group - LAG)
    for group in range(groups - LAG, groups):
        finish(group)
    for copy in out:
        copy.wait()


def scratch_of(item):
    if isinstance(item, tuple):
        return pltpu.VMEM(*item) if isinstance(item[0], tuple) else pltpu.VMEM(item, F32)
    return item


def call(kernel, ins, outs, scratch, work, vmem=16):
    return pl.pallas_call(
        kernel,
        out_shape=[jax.ShapeDtypeStruct(*out[:2]) for out in outs],
        in_specs=[pl.BlockSpec(memory_space=space) for _, space in ins],
        out_specs=[pl.BlockSpec(memory_space=(*out, pltpu.VMEM)[2]) for out in outs],
        scratch_shapes=[scratch_of(item) for item in scratch],
        compiler_params=pltpu.CompilerParams(vmem_limit_bytes=vmem * 1024 * 1024),
        cost_estimate=pl.CostEstimate(flops=work, bytes_accessed=work // 8, transcendentals=0),
    )(*[array for array, _ in ins])


def on_device(
    query_feat,
    key_feat,
    value_feat,
    decay_rate,
    residues,
    skip_gain,
    norm_gain,
    doc_starts,
    cotangent,
):
    tokens, width = query_feat.shape
    parts, peers = lax.axis_size("seq"), lax.axis_size("chan")
    tiles, groups = tokens // TILE, width // LANES
    starts = (doc_starts, pltpu.SMEM)
    weight = residues * jnp.sqrt(-jnp.expm1(-2.0 * decay_rate))
    skip, gain = skip_gain[None], norm_gain[None]
    whole, split, pitched = (tokens, width), (groups, tokens, LANES), (groups, tiles * PITCH, LANES)
    block, spread, summed = (parts, groups * MODES, LANES), (tokens, LANES), (peers, ROWS, LANES)
    modes, packed = (MODES, width), (table_rows(tiles, groups, parts), LANES)
    head_split, tail_split = (HEAD, tokens, LANES), (groups - HEAD, tokens, LANES)
    work = tokens * width

    def vmem(*arrays):
        return [(array, pltpu.VMEM) for array in arrays]

    def hbm(*arrays):
        return [(array, pl.ANY) for array in arrays]

    def sems(count):
        return pltpu.SemaphoreType.DMA((count,))

    (send,) = call(
        first_kernel,
        hbm(doc_starts, key_feat, value_feat, decay_rate),
        [(block, SEND)],
        [
            pltpu.SMEM(doc_starts.shape, jnp.int32),
            (split, BF16),
            (split, BF16),
            modes,
            sems(2 * groups + 2),
        ],
        work * 20,
        60,
    )
    got = lax.all_to_all(send, "seq", 0, 0)
    conv, table = call(
        forward_local_kernel,
        [starts] + vmem(key_feat, value_feat, decay_rate, weight, gain, skip),
        [(split, F32), (packed, F32)],
        [pitched, pitched],
        work * 50,
    )
    mixer, sums = call(
        forward_join_kernel,
        vmem(table, got, conv, query_feat, cotangent),
        [(whole, BF16), (summed, F32)],
        [spread, spread],
        work * 30,
    )
    sums = lax.all_to_all(sums, "chan", 0, 0)
    adjoint, send, totals = call(
        backward_kernel,
        vmem(table, sums, query_feat, cotangent, mixer),
        [(whole, BF16), (block, SEND), ((ROWS, LANES), F32)],
        [spread, spread],
        work * 30,
    )
    got = lax.all_to_all(send, "seq", 0, 0)
    mixed, grad_query, done = call(
        outputs_kernel,
        vmem(table, totals, query_feat, cotangent, mixer),
        [(whole, BF16), (whole, BF16), ((ROWS, LANES), F32)],
        [spread, spread],
        work * 20,
    )
    head, tail, flags = call(
        backward_local_kernel,
        [starts] + vmem(table, adjoint, done),
        [(head_split, F32), (tail_split, F32), ((2 * parts, LANES), F32)],
        [pitched, pitched],
        work * 50,
    )
    grad_key, grad_value = call(
        backward_join_kernel,
        vmem(table, flags, got, head, tail) + hbm(key_feat, value_feat),
        [(whole, BF16, pl.ANY), (whole, BF16, pl.ANY)],
        [(split, BF16)] * 5 + [sems(4 * groups)],
        work * 30,
        52,
    )
    return mixed, grad_query, grad_key, grad_value


def solution(mesh):
    both = P("seq", "chan")
    in_specs = (
        both,
        both,
        both,
        P(None, "chan"),
        P(None, "chan"),
        P("chan"),
        P("chan"),
        P(),
        both,
    )
    return jax.shard_map(
        on_device, mesh=mesh, in_specs=in_specs, out_specs=(both,) * 4, check_vma=False
    )
```
